256 devices in a mesh: gx: 32 (over y_hi, z, core), gy: 8 (over y_lo, x).
Axes of the slice: x: 4, y: 4 (y_hi: 2, y_lo: 2; y = y_hi * 2 + y_lo), z: 8, core: 2. Of those that a mesh axis runs over, the one named last changes fastest.
Arguments:
- check_state: float32 [4, 288, 288, 192], P(None, 'gx', 'gy'), may hold values from -6 to 6
- syndrome: int32 [4, 288, 288], P(None, 'gx', 'gy'), may hold values 0 or 1
- left_state: float32 [4, 288, 288, 192], P(None, 'gx', 'gy'), may hold values from -6 to 6
- right_state: float32 [4, 288, 288, 192], P(None, 'gx', 'gy'), may hold values from -6 to 6
- offsets_one: int32 [6, 2], replicated, may hold values from -3 to 3, as said below
- offsets_two: int32 [6, 2], replicated, may hold values from -3 to 3, as said below
- syndrome_gain: float32 [192], replicated, may hold values from -6 to 6
- mix_one: float32 [6, 192, 192], replicated, may hold values from -0.4375 to 0.4375
- grow_one: float32 [2, 384, 384], replicated, may hold values from -0.3125 to 0.3125
- shrink_one: float32 [2, 384, 192], replicated, may hold values from -0.3125 to 0.3125
- mix_two: float32 [6, 192, 192], replicated, may hold values from -0.4375 to 0.4375
- grow_two: float32 [384, 384], replicated, may hold values from -0.3125 to 0.3125
- shrink_two: float32 [384, 192], replicated, may hold values from -0.3125 to 0.3125
Outputs:
- left_out: float32 [4, 288, 288, 192], P(None, 'gx', 'gy')
- right_out: float32 [4, 288, 288, 192], P(None, 'gx', 'gy')
- check_out: float32 [4, 288, 288, 192], P(None, 'gx', 'gy')
The draws below stay inside these ranges and needn't reach their ends.
Inputs may be any that keep to these rules, and one draw needn't show every extreme that they name: `offsets_one`: each component of every offset lies between -3 and 3; in each layer and each of the two components, both ends are taken by some offset. `offsets_two`: each component of every offset lies between -3 and 3; in each layer and each of the two components, both ends are taken by some offset.
All inputs are finite; a program needn't handle non-finite values. No bound on the sum of `syndrome` on one device may be relied on, other than what follows from the above.
Results may differ from the reference program's by a relative error of at most 0.0001.
Values sent between devices are 32-bit elements; how exact they have to be, the bound alone decides.
No kernel may reach another device: no remote copies, remote signals or barrier semaphores. Data moves between devices by JAX's collectives and lax.ppermute only.
A program may use at most 128 MiB of HBM per device.

```python
import jax
import jax.numpy as jnp
from jax import lax

C = 192
SPAN = 3
SHOTS = 4
NX = 288
NY = 288


def spread_offsets(key):
    values = jax.random.randint(jax.random.fold_in(key, 1), (6, 2), -SPAN, SPAN + 1, dtype=jnp.int32)
    order = jax.random.permutation(jax.random.fold_in(key, 2), 6)
    values = values.at[order[0], 0].set(SPAN)
    values = values.at[order[1], 0].set(-SPAN)
    values = values.at[order[2], 1].set(SPAN)
    values = values.at[order[3], 1].set(-SPAN)
    return values


def draw_offsets_one(key, part):
    key = jax.random.fold_in(key, 11)
    return spread_offsets(key)


def draw_offsets_two(key, part):
    key = jax.random.fold_in(key, 23)
    return spread_offsets(key)


def plant(values, key, smallest, largest):
    longest = values.shape.index(max(values.shape))
    spots = []
    for shift in (0, 1):
        where = [jax.random.randint(jax.random.fold_in(key, axis), (), 0, length) for axis, length in enumerate(values.shape)]
        where[longest] = (where[longest] + shift) % values.shape[longest]
        spots.append(tuple(where))
    return values.at[spots[0]].set(smallest).at[spots[1]].set(largest)


def steps_of(stream_key, shape, cuts, smallest, high):
    gain = 1.0
    for dim, parts in cuts:
        steps = jax.random.uniform(jax.random.fold_in(jax.random.fold_in(stream_key, 6), dim), (parts,), jnp.float32, smallest / len(cuts), high / len(cuts))
        gain = gain * jnp.repeat(jnp.exp(steps), shape[dim] // parts).reshape((-1,) + (1,) * (len(shape) - 1 - dim))
    return gain


def gaussian(rng, dims, scale, reach, pieces=(), kind=jnp.bfloat16):
    array = jax.random.normal(rng, dims, jnp.float32) * scale
    if len(pieces) > 0:
        array = steps_of(rng, dims, pieces, -0.22, 0.18) * array
    return jnp.clip(array, min=-reach, max=reach).astype(kind)


def setup_inputs(seed: int = 0) -> dict:
    streams_of = jax.random.split(jax.random.key(seed), 14)
    check_state = gaussian(streams_of[0], (SHOTS, NX, NY, C), 1.0, 6.0, ((1, 32), (2, 8)), jnp.float32)
    syndrome = plant((jax.random.randint(streams_of[1], (SHOTS, NX, NY), 0, 4) < 1).astype(jnp.int32), jax.random.fold_in(streams_of[1], 1), 0, 1)
    left_state = gaussian(streams_of[2], (SHOTS, NX, NY, C), 1.0, 6.0, ((1, 32), (2, 8)), jnp.float32)
    right_state = gaussian(streams_of[3], (SHOTS, NX, NY, C), 1.0, 6.0, ((1, 32), (2, 8)), jnp.float32)
    offsets_one = draw_offsets_one(jax.random.fold_in(streams_of[13], 71), 0)
    offsets_two = draw_offsets_two(jax.random.fold_in(streams_of[13], 71), 0)
    syndrome_gain = gaussian(streams_of[6], (C,), 1.0, 6.0, (), jnp.float32)
    mix_one = gaussian(streams_of[7], (6, C, C), C ** -0.5, 0.4375, (), jnp.float32)
    grow_one = gaussian(streams_of[8], (2, 2 * C, 2 * C), (2 * C) ** -0.5, 0.3125, (), jnp.float32)
    shrink_one = gaussian(streams_of[9], (2, 2 * C, C), (2 * C) ** -0.5, 0.3125, (), jnp.float32)
    mix_two = gaussian(streams_of[10], (6, C, C), C ** -0.5, 0.4375, (), jnp.float32)
    grow_two = gaussian(streams_of[11], (2 * C, 2 * C), (2 * C) ** -0.5, 0.3125, (), jnp.float32)
    shrink_two = gaussian(streams_of[12], (2 * C, C), (2 * C) ** -0.5, 0.3125, (), jnp.float32)
    return dict(check_state=check_state, syndrome=syndrome, left_state=left_state, right_state=right_state, offsets_one=offsets_one, offsets_two=offsets_two, syndrome_gain=syndrome_gain, mix_one=mix_one, grow_one=grow_one, shrink_one=shrink_one, mix_two=mix_two, grow_two=grow_two, shrink_two=shrink_two)


def shifted(field, offset):
    return jnp.roll(field, (-offset[0], -offset[1]), axis=(0, 1))

def mixed(field, offsets, weights):
    total = None
    for k in range(offsets.shape[0]):
        slab = shifted(field, offsets[k])
        term = jnp.dot(slab.reshape(-1, slab.shape[-1]), weights[k], precision=lax.Precision.HIGHEST, preferred_element_type=jnp.float32)
        total = term if total is None else total + term
    return total.reshape(field.shape)

def update(state, message, grow, shrink):
    joined = jnp.concatenate([state, message], axis=-1)
    flat = joined.reshape(-1, joined.shape[-1])
    scaled = flat * lax.rsqrt(lax.optimization_barrier(jnp.mean(flat * flat, axis=-1, keepdims=True)) + 1e-05)
    inner = jax.nn.silu(jnp.dot(scaled, grow, precision=lax.Precision.HIGHEST, preferred_element_type=jnp.float32))
    branch = jnp.dot(inner, shrink, precision=lax.Precision.HIGHEST, preferred_element_type=jnp.float32)
    return state + branch.reshape(state.shape)

def reference(check_state, syndrome, left_state, right_state, offsets_one, offsets_two, syndrome_gain, mix_one, grow_one, shrink_one, mix_two, grow_two, shrink_two):

    def one_shot(items):
        check_now, bits, left_now, right_now = items
        checks = check_now + (2 * bits - 1).astype(check_now.dtype)[..., None] * syndrome_gain
        left_new = update(left_now, mixed(checks, offsets_one[0:3], mix_one[0:3]), grow_one[0], shrink_one[0])
        right_new = update(right_now, mixed(checks, offsets_one[3:6], mix_one[3:6]), grow_one[1], shrink_one[1])
        gathered = mixed(left_new, offsets_two[0:3], mix_two[0:3]) + mixed(right_new, offsets_two[3:6], mix_two[3:6])
        check_new = update(checks, gathered, grow_two, shrink_two)
        return (left_new, right_new, check_new)
    left_out, right_out, check_out = lax.map(one_shot, (check_state, syndrome, left_state, right_state))
    return (left_out, right_out, check_out)
```

```python
import jax
import jax.numpy as jnp
from jax import lax
from jax.experimental import pallas as pl
from jax.experimental.pallas import tpu as pltpu
from jax.sharding import PartitionSpec as P

SPAN = 3
C = 192
F32 = jnp.float32
BF16 = jnp.bfloat16


GROUP = 3


def split(x):
    hi = x.astype(BF16)
    lo = (x - hi.astype(F32)).astype(BF16)
    return hi, lo


def packed(x):
    first, rest = x[:, :128], x[:, 128:]
    hi, lo = split(first)
    twice = jnp.concatenate([rest, rest], axis=1)
    rest_hi = twice.astype(BF16).astype(F32)
    lane = lax.broadcasted_iota(jnp.int32, twice.shape, 1)
    both = jnp.where(lane < 64, rest_hi, twice - rest_hi).astype(BF16)
    return [hi, both, lo]


def dot(a, b):
    return lax.dot_general(a, b, (((1,), (0,)), ((), ())), preferred_element_type=F32)


def dot_t(a, b):
    return lax.dot_general(a, b, (((1,), (1,)), ((), ())), preferred_element_type=F32)


def silu(v):
    return 0.5 * v * (1.0 + jnp.tanh(0.5 * v))


def vmem(count):
    return [pl.BlockSpec(memory_space=pltpu.VMEM)] * count


PARAMS = dict(compiler_params=pltpu.CompilerParams(vmem_limit_bytes=48 * 1024 * 1024))


def pair_rows(out, at, weights):
    hi, lo = split(weights)
    out[at : at + 192, :] = hi
    out[at + 192 : at + 256, :] = hi[128:192]
    out[at + 256 : at + 384, :] = hi[0:128]
    return lo


def low_rows(out, at, lo):
    out[at : at + 192, :] = lo
    out[at + 192 : at + 256, :] = jnp.zeros((64, lo.shape[1]), BF16)


def weights_kernel(mix_one, grow_one, shrink_one, mix_two, grow_two, shrink_two, m1, g1, s1, m2, g2, s2):
    def grow(src, out):
        low = pair_rows(out, 0, src[0:192, :])
        low_rows(out, 768, low)
        low = pair_rows(out, 384, src[192:384, :])
        low_rows(out, 1024, low)

    def shrink(src, out):
        hi, lo = split(src[...])
        out[:, 0:384] = hi
        out[:, 384:768] = hi
        out[:, 768:1152] = lo

    for b in range(2):
        for k in range(3):
            low = pair_rows(m1.at[b], 384 * k, mix_one[3 * b + k])
            low_rows(m1.at[b], 1152 + 256 * k, low)
            low = pair_rows(m2.at[3 * b + k], 0, mix_two[3 * b + k])
            low_rows(m2.at[3 * b + k], 384, low)
        grow(grow_one.at[b], g1.at[b])
        shrink(shrink_one.at[b], s1.at[b])
    grow(grow_two, g2)
    shrink(shrink_two, s2)


def prepare_weights(mix_one, grow_one, shrink_one, mix_two, grow_two, shrink_two):
    shapes = [(2, 1920, 192), (2, 1280, 384), (2, 192, 1152), (6, 640, 192), (1280, 384), (192, 1152)]
    return pl.pallas_call(
        weights_kernel,
        out_shape=[jax.ShapeDtypeStruct(s, BF16) for s in shapes],
        in_specs=vmem(6),
        out_specs=vmem(6),
        name="weights",
        **PARAMS,
    )(mix_one, grow_one, jnp.swapaxes(shrink_one, 1, 2), mix_two, grow_two, shrink_two.T)


def checks_kernel(check, syndrome, gain, checks, top, bottom):
    column = lax.broadcasted_iota(jnp.int32, (36, 8, 36), 0)
    lane = lax.broadcasted_iota(jnp.int32, (36, 8, 36), 2)
    pick = (column == lane).astype(F32)
    for r in range(9):
        bits = (2 * syndrome[r] - 1).astype(F32)
        bits = jnp.concatenate([bits, bits], axis=0)
        sign = jnp.sum(pick * bits[None], axis=-1, keepdims=True)[:, 0:4, :]
        value = check[r] + sign * gain[...]
        checks[r] = value
        if r < 3:
            top[r] = value
        if r >= 6:
            bottom[r - 6] = value


def make_checks(check, syndrome, gain):
    edge = jax.ShapeDtypeStruct((3, 36, 4, C), F32)
    return pl.pallas_call(
        checks_kernel,
        out_shape=[jax.ShapeDtypeStruct((9, 36, 4, C), F32), edge, edge],
        in_specs=vmem(3),
        out_specs=vmem(3),
        name="checks",
        **PARAMS,
    )(check, syndrome, gain)


def update(h, m, grow, shrink):
    mean = jnp.sum(h * h + m * m, axis=-1, keepdims=True) * (1.0 / 384.0)
    hp, mp = packed(h), packed(m)
    z = jnp.concatenate(hp + mp + hp[:2] + mp[:2], axis=1)
    inner = silu(dot(z, grow[...]) * lax.rsqrt(mean + 1e-05))
    hi, lo = split(inner)
    return h + dot_t(jnp.concatenate([hi, lo, hi], axis=1), shrink[...])


def layer_one_kernel(
    off_one, off_two, checks, top, bottom, west, east, left, right, m1, g1, s1, m2,
    left_out, right_out, acc_mid, acc_top, acc_bottom, acc_west, acc_east, checks_q,
    field, pairs, acc, state, fresh,
):
    for q in range(4):
        sub = slice(4 * q, 4 * q + 4)
        lo_j, hi_j = (3 if q == 0 else 0), (12 if q == 3 else 15)
        cols = slice(9 * q + lo_j - 3, 9 * q + hi_j - 3)
        field[0:3, lo_j:hi_j, sub, :] = top[:, cols]
        field[3:12, lo_j:hi_j, sub, :] = checks[:, cols]
        field[12:15, lo_j:hi_j, sub, :] = bottom[:, cols]
        for b, ref in enumerate((left, right)):
            state[b, :, :, sub, :] = ref[:, 9 * q : 9 * q + 9]
    field[:, 0:3, 0:4, :] = west[...]
    field[:, 12:15, 12:16, :] = east[...]

    def pack_row(r, carry):
        tiles = packed(field[r].reshape(240, C))
        for t in range(3):
            pairs[r, :, :, 128 * t : 128 * t + 128] = tiles[t].reshape(15, 16, 128)
        return carry

    lax.fori_loop(0, 15, pack_row, 0)
    checks_q[...] = field[3:12, 3:12]
    acc[...] = jnp.zeros(acc.shape, F32)

    size = GROUP * 9 * 16

    def group(g, carry):
        row = g * GROUP
        for b in range(2):
            slabs = [
                pairs[
                    pl.ds(row + SPAN + off_one[3 * b + k, 0], GROUP), pl.ds(SPAN + off_one[3 * b + k, 1], 9)
                ].reshape(size, 384)
                for k in range(3)
            ]
            lhs = jnp.concatenate(slabs + [s[:, :256] for s in slabs], axis=1)
            m = dot(lhs, m1[b])
            h = state[b, pl.ds(row, GROUP)].reshape(size, C)
            new = update(h, m, g1.at[b], s1.at[b])
            fresh[b, pl.ds(row, GROUP)] = new.reshape(GROUP, 9, 16, C)
            tiles = packed(new)
            lhs = jnp.concatenate(tiles + tiles[:2], axis=1)
            for k in range(3):
                part = dot(lhs, m2[3 * b + k]).reshape(GROUP, 9, 16, C)
                where = (
                    pl.ds(row + SPAN - off_two[3 * b + k, 0], GROUP),
                    pl.ds(SPAN - off_two[3 * b + k, 1], 9),
                )
                acc[where] = acc[where] + part
        return carry

    lax.fori_loop(0, 9 // GROUP, group, 0)

    for b, ref in enumerate((left_out, right_out)):
        for q in range(4):
            ref[:, 9 * q : 9 * q + 9] = fresh[b, :, :, 4 * q : 4 * q + 4, :]
    for q in range(3):
        low, high = slice(4 * q, 4 * q + 4), slice(4 * q + 4, 4 * q + 8)
        acc[:, 3:6, high, :] = acc[:, 3:6, high, :] + acc[:, 12:15, low, :]
        acc[:, 9:12, low, :] = acc[:, 9:12, low, :] + acc[:, 0:3, high, :]
    acc_mid[...] = acc[3:12, 3:12]
    for ref, rows in ((acc_top, slice(0, 3)), (acc_bottom, slice(12, 15))):
        ref[:, 0:3] = acc[rows, 0:3, 0:4, :]
        for q in range(4):
            ref[:, 3 + 9 * q : 12 + 9 * q] = acc[rows, 3:12, 4 * q : 4 * q + 4, :]
        ref[:, 39:42] = acc[rows, 12:15, 12:16, :]
    acc_west[...] = acc[3:12, 0:3, 0:4, :]
    acc_east[...] = acc[3:12, 12:15, 12:16, :]


def layer_one(*operands):
    shapes = [
        (9, 36, 4, C), (9, 36, 4, C), (9, 9, 16, C), (3, 42, 4, C), (3, 42, 4, C), (9, 3, 4, C), (9, 3, 4, C),
        (9, 9, 16, C),
    ]
    smem = pl.BlockSpec(memory_space=pltpu.SMEM)
    return pl.pallas_call(
        layer_one_kernel,
        out_shape=[jax.ShapeDtypeStruct(s, F32) for s in shapes],
        in_specs=[smem, smem] + vmem(11),
        out_specs=vmem(8),
        scratch_shapes=[
            pltpu.VMEM((15, 15, 16, C), F32),
            pltpu.VMEM((15, 15, 16, 384), BF16),
            pltpu.VMEM((15, 15, 16, C), F32),
            pltpu.VMEM((2, 9, 9, 16, C), F32),
            pltpu.VMEM((2, 9, 9, 16, C), F32),
        ],
        name="layer_one",
        **PARAMS,
    )(*operands)


def layer_two_kernel(acc_mid, from_top, from_bottom, from_west, from_east, checks_q, g2, s2, out, acc, fresh):
    acc[...] = acc_mid[...]
    for q in range(4):
        sub = slice(4 * q, 4 * q + 4)
        cols = slice(3 + 9 * q, 12 + 9 * q)
        acc[0:3, :, sub, :] = acc[0:3, :, sub, :] + from_top[:, cols]
        acc[6:9, :, sub, :] = acc[6:9, :, sub, :] + from_bottom[:, cols]
    acc[:, 0:3, 0:4, :] = acc[:, 0:3, 0:4, :] + from_west[...]
    acc[:, 6:9, 12:16, :] = acc[:, 6:9, 12:16, :] + from_east[...]
    size = GROUP * 9 * 16

    def group(g, carry):
        rows = pl.ds(g * GROUP, GROUP)
        new = update(checks_q[rows].reshape(size, C), acc[rows].reshape(size, C), g2, s2)
        fresh[rows] = new.reshape(GROUP, 9, 16, C)
        return carry

    lax.fori_loop(0, 9 // GROUP, group, 0)
    for q in range(4):
        out[:, 9 * q : 9 * q + 9] = fresh[:, :, 4 * q : 4 * q + 4, :]


def layer_two(*operands):
    return pl.pallas_call(
        layer_two_kernel,
        out_shape=jax.ShapeDtypeStruct((9, 36, 4, C), F32),
        in_specs=vmem(8),
        out_specs=pl.BlockSpec(memory_space=pltpu.VMEM),
        scratch_shapes=[pltpu.VMEM((9, 9, 16, C), F32), pltpu.VMEM((9, 9, 16, C), F32)],
        name="layer_two",
        **PARAMS,
    )(*operands)


def ring(axis):
    count = lax.axis_size(axis)
    up = [(i, (i + 1) % count) for i in range(count)]
    return up, [(b, a) for a, b in up]


def exchange(axis, low, high):
    up, down = ring(axis)
    return lax.ppermute(high, axis, up), lax.ppermute(low, axis, down)


def body(
    check_state, syndrome, left_state, right_state, offsets_one, offsets_two, syndrome_gain,
    mix_one, grow_one, shrink_one, mix_two, grow_two, shrink_two,
):
    site = lambda x: jnp.transpose(x, (1, 2, 0, 3))
    back = lambda x: jnp.transpose(x, (2, 0, 1, 3))
    checks, first, last = make_checks(
        site(check_state), jnp.transpose(syndrome, (1, 0, 2)), syndrome_gain.reshape(1, C)
    )
    top, bottom = exchange("gx", first, last)
    m1, g1, s1, m2, g2, s2 = prepare_weights(mix_one, grow_one, shrink_one, mix_two, grow_two, shrink_two)
    edge = lambda part: jnp.concatenate([top[:, part], checks[:, part], bottom[:, part]], axis=0)
    west, east = exchange("gy", edge(slice(0, 3)), edge(slice(33, 36)))
    left_out, right_out, acc_mid, acc_top, acc_bottom, acc_west, acc_east, checks_q = layer_one(
        offsets_one, offsets_two, checks, top, bottom, west, east, site(left_state), site(right_state), m1, g1, s1, m2
    )
    from_top, from_bottom = exchange("gx", acc_top, acc_bottom)

    def side(mid, cols):
        return jnp.concatenate([mid[0:3] + from_top[:, cols], mid[3:6], mid[6:9] + from_bottom[:, cols]], axis=0)

    from_west, from_east = exchange("gy", side(acc_west, slice(0, 3)), side(acc_east, slice(39, 42)))
    check_out = layer_two(acc_mid, from_top, from_bottom, from_west, from_east, checks_q, g2, s2)
    return back(left_out), back(right_out), back(check_out)


def solution(mesh):
    site = P(None, "gx", "gy", None)
    in_specs = (site, P(None, "gx", "gy"), site, site) + (P(),) * 9
    return jax.shard_map(body, mesh=mesh, in_specs=in_specs, out_specs=(site,) * 3, check_vma=False)
```

```python
import jax
import jax.numpy as jnp
from jax import lax
from jax.experimental import pallas as pl
from jax.experimental.pallas import tpu as pltpu
from jax.sharding import PartitionSpec as P

SPAN = 3
C = 192
F32 = jnp.float32
BF16 = jnp.bfloat16


def split(x):
    hi = x.astype(BF16)
    lo = (x - hi.astype(F32)).astype(BF16)
    return hi, lo


def packed(x):
    first, rest = x[:, :128], x[:, 128:]
    hi, lo = split(first)
    twice = jnp.concatenate([rest, rest], axis=1)
    rest_hi = twice.astype(BF16).astype(F32)
    lane = lax.broadcasted_iota(jnp.int32, twice.shape, 1)
    both = jnp.where(lane < 64, rest_hi, twice - rest_hi).astype(BF16)
    return [hi, both, lo]


def dot(a, b):
    return lax.dot_general(a, b, (((1,), (0,)), ((), ())), preferred_element_type=F32)


def dot_t(a, b):
    return lax.dot_general(a, b, (((1,), (1,)), ((), ())), preferred_element_type=F32)


def silu(v):
    return 0.5 * v * (1.0 + jnp.tanh(0.5 * v))


def vmem(count):
    return [pl.BlockSpec(memory_space=pltpu.VMEM)] * count


def params(mib):
    return pltpu.CompilerParams(vmem_limit_bytes=mib * 1024 * 1024)


HBM = pl.BlockSpec(memory_space=pltpu.HBM)


def far_off(*arrays):
    return [pltpu.with_memory_space_constraint(x, pltpu.HBM) for x in arrays]


def results(shapes, kind=F32):
    return [jax.ShapeDtypeStruct(shape, kind) for shape in shapes]


def fetch(pairs, sems):
    copies = [pltpu.make_async_copy(src, dst, sems.at[i]) for i, (src, dst) in enumerate(pairs)]
    for copy in copies:
        copy.start()
    return copies


def pair_rows(out, weights):
    hi, lo = split(weights)
    n = weights.shape[1]
    out[0:192, :n] = hi
    out[192:256, :n] = hi[128:192]
    out[256:384, :n] = hi[0:128]
    return lo


def low_rows(out, lo):
    n = lo.shape[1]
    out[0:192, :n] = lo
    out[192:256, :n] = jnp.zeros((64, n), BF16)


def picker():
    column = lax.broadcasted_iota(jnp.int32, (36, 8, 36), 0)
    lane = lax.broadcasted_iota(jnp.int32, (36, 8, 36), 2)
    return (column == lane).astype(F32)


def checks_row(check, syndrome, gain, pick):
    bits = (2 * syndrome - 1).astype(F32)
    bits = jnp.concatenate([bits, bits], axis=0)
    sign = jnp.sum(pick * bits[None], axis=-1, keepdims=True)[:, 0:4, :]
    return check + sign * gain


def is_odd():
    return lax.rem(lax.axis_index("gx"), 2)


def dense(value):
    half = value.shape[1] // 2
    rest = jnp.concatenate([value[:, :half, :, 128:], value[:, half:, :, 128:]], axis=-1)
    return jnp.concatenate([value[:, :, :, :128], rest], axis=1)


def undense(out, ref):
    columns = out.shape[1]
    half = columns // 2
    out[:, :, :, :128] = ref[:, :columns]
    out[:, :half, :, 128:] = ref[:, columns:, :, :64]
    out[:, half:, :, 128:] = ref[:, columns:, :, 64:]


def edges_kernel(check, syndrome, gain, near, far, first, last, rows, bits, gains, sems):
    copies = fetch(
        [(syndrome, bits), (gain, gains)] + [(check.at[r], rows.at[r]) for r in (0, 1, 2, 6, 7, 8)], sems
    )
    pick = picker()
    copies[0].wait()
    copies[1].wait()
    for n, r in enumerate((0, 1, 2, 6, 7, 8)):
        copies[2 + n].wait()
        value = checks_row(rows[r], bits[r], gains[...], pick)
        if r < 3:
            first[r] = value
        else:
            last[r - 6] = value
    odd = is_odd() == 1
    low, high = dense(first[...]), dense(last[...])
    near[...] = jnp.where(odd, low, high)
    far[...] = jnp.where(odd, high, low)


def make_edges(check, syndrome, gain):
    return pl.pallas_call(
        edges_kernel,
        out_shape=results([(3, 54, 4, 128)] * 2 + [(3, 36, 4, C)] * 2),
        in_specs=[HBM] * 3,
        out_specs=vmem(4),
        scratch_shapes=[
            pltpu.VMEM((9, 36, 4, C), F32), pltpu.VMEM((9, 4, 36), jnp.int32), pltpu.VMEM((1, C), F32),
            pltpu.SemaphoreType.DMA((8,)),
        ],
        name="edges",
        compiler_params=params(8),
    )(*far_off(check, syndrome, gain))


def prework_kernel(
    check, syndrome, gain, left, right, mix_one, grow_one, shrink_one, mix_two, grow_two, shrink_two,
    middle, m1, g1m, s1, m2, g2h, g2m, s2, left_q, right_q, left_g, right_g,
    g1h, rows, bits, gains, lefts, rights, mix_1, grow_1, shrink_1, mix_2, grow_2, shrink_2, sems,
):
    copies = fetch(
        [
            (left, lefts), (grow_one, grow_1), (right, rights), (mix_one, mix_1), (mix_two, mix_2),
            (shrink_one, shrink_1), (grow_two, grow_2), (shrink_two, shrink_2),
            (syndrome, bits), (gain, gains), (check.at[3:6], rows),
        ],
        sems,
    )

    def grow(src, out_h, out_m):
        for at, out in ((0, out_h), (192, out_m)):
            low_rows(out.at[384:640], pair_rows(out.at[0:384], src[at : at + 192, :]))

    def shrink(src, out):
        hi, lo = split(src[...])
        out[:, 0:384] = hi
        out[:, 384:768] = hi
        out[:, 768:1152] = lo

    for b, (ref, quart, half) in enumerate(((lefts, left_q, left_g), (rights, right_q, right_g))):
        copies[2 * b].wait()
        for q in range(4):
            quart[:, :, 4 * q : 4 * q + 4, :] = ref[:, 9 * q : 9 * q + 9]
        if b == 0:
            copies[1].wait()
        grow(grow_1.at[b], g1h, g1m.at[b])
        tiles = packed(quart[...].reshape(1296, C))
        half[...] = dot(jnp.concatenate(tiles + tiles[:2], axis=1), g1h[...]).reshape(9, 144, 384)
    copies[3].wait()
    copies[4].wait()
    copies[5].wait()
    for b in range(2):
        for k in range(3):
            low = pair_rows(m1.at[b, 384 * k : 384 * k + 384], mix_1[3 * b + k])
            low_rows(m1.at[b, 1152 + 256 * k : 1408 + 256 * k], low)
            out = m2.at[b, :, 256 * k : 256 * k + 256]
            low_rows(out.at[384:640], pair_rows(out.at[0:384], mix_2[3 * b + k]))
        shrink(shrink_1.at[b], s1.at[b])
    for copy in copies[6:]:
        copy.wait()
    grow(grow_2, g2h, g2m)
    shrink(shrink_2, s2)
    pick = picker()
    for r in range(3):
        middle[r] = checks_row(rows[r], bits[3 + r], gains[...], pick)


def prework(*operands):
    weights = [(2, 1920, C), (2, 640, 384), (2, C, 1152), (2, 640, 768), (640, 384), (640, 384), (C, 1152)]
    states = [(9, 9, 16, C)] * 2 + [(9, 144, 384)] * 2
    scratch = [(3, 36, 4, C), (9, 4, 36), (1, C), (9, 36, 4, C), (9, 36, 4, C), (6, C, C), (2, 384, 384)]
    scratch += [(2, C, 384), (6, C, C), (384, 384), (C, 384)]
    return pl.pallas_call(
        prework_kernel,
        out_shape=results([(3, 36, 4, C)]) + results(weights, BF16) + results(states),
        in_specs=[HBM] * 11,
        out_specs=vmem(12),
        scratch_shapes=[pltpu.VMEM((640, 384), BF16)]
        + [pltpu.VMEM(s, jnp.int32 if s == (9, 4, 36) else F32) for s in scratch]
        + [pltpu.SemaphoreType.DMA((11,))],
        name="prework",
        compiler_params=params(14),
    )(*far_off(*operands))


def columns_kernel(first, middle, last, near, far, low, high, top, bottom, rows):
    undense(rows.at[0], near)
    undense(rows.at[1], far)
    odd = is_odd()
    top[...] = rows[1 - odd]
    bottom[...] = rows[odd]
    for r, ref in enumerate((top, first, middle, last, bottom)):
        low[3 * r : 3 * r + 3] = ref[:, 0:3]
        high[3 * r : 3 * r + 3] = ref[:, 33:36]


def make_columns(*operands):
    return pl.pallas_call(
        columns_kernel,
        out_shape=results([(15, 3, 4, C)] * 2 + [(3, 36, 4, C)] * 2),
        in_specs=vmem(5),
        out_specs=vmem(4),
        scratch_shapes=[pltpu.VMEM((2, 3, 36, 4, C), F32)],
        name="columns",
        compiler_params=params(6),
    )(*operands)


def sums_kernel(acc_west, acc_east, near, far, low, high, top, bottom, rows):
    undense(rows.at[0], near)
    undense(rows.at[1], far)
    odd = is_odd()
    top[...] = rows[1 - odd]
    bottom[...] = rows[odd]
    for ref, acc, cols in ((low, acc_west, slice(0, 3)), (high, acc_east, slice(39, 42))):
        ref[0:3] = acc[0:3] + top[:, cols]
        ref[3:6] = acc[3:6]
        ref[6:9] = acc[6:9] + bottom[:, cols]


def make_sums(*operands):
    return pl.pallas_call(
        sums_kernel,
        out_shape=results([(9, 3, 4, C)] * 2 + [(3, 42, 4, C)] * 2),
        in_specs=vmem(4),
        out_specs=vmem(4),
        scratch_shapes=[pltpu.VMEM((2, 3, 42, 4, C), F32)],
        name="sums",
        compiler_params=params(6),
    )(*operands)


def fields_kernel(first, middle, last, top, bottom, g2h, pairs, west_q, east_q, checks_q, checks_g, field):
    for q in range(4):
        sub = slice(4 * q, 4 * q + 4)
        lo_j, hi_j = (3 if q == 0 else 0), (12 if q == 3 else 15)
        cols = slice(9 * q + lo_j - 3, 9 * q + hi_j - 3)
        for r, ref in enumerate((top, first, middle, last, bottom)):
            field[3 * r : 3 * r + 3, lo_j:hi_j, sub, :] = ref[:, cols]
    west_q[...] = field[:, 0:3]
    east_q[...] = field[:, 12:15]
    checks_q[...] = field[3:12, 3:12]
    tiles = packed(field[:, 3:12].reshape(2160, C))
    for t in range(3):
        pairs[:, :, :, 128 * t : 128 * t + 128] = tiles[t].reshape(15, 9, 16, 128)
    mid = pairs[3:12].reshape(1296, 384)
    checks_g[...] = dot(jnp.concatenate([mid, mid[:, :256]], axis=1), g2h[...])


def make_fields(first, middle, last, top, bottom, g2h):
    shapes = [(15, 3, 16, C), (15, 3, 16, C), (9, 9, 16, C), (1296, 384)]
    return pl.pallas_call(
        fields_kernel,
        out_shape=results([(15, 9, 16, 384)], BF16) + results(shapes),
        in_specs=vmem(6),
        out_specs=vmem(5),
        scratch_shapes=[pltpu.VMEM((15, 15, 16, C), F32)],
        name="fields",
        compiler_params=params(10),
    )(first, middle, last, top, bottom, g2h)


def update(h, half, m, grow, shrink):
    mean = jnp.sum(h * h + m * m, axis=-1, keepdims=True) * (1.0 / 384.0)
    mp = packed(m)
    inner = silu((dot(jnp.concatenate(mp + mp[:2], axis=1), grow[...]) + half) * lax.rsqrt(mean + 1e-05))
    hi, lo = split(inner)
    return h + dot_t(jnp.concatenate([hi, lo, hi], axis=1), shrink[...])


def block_step(b, starts, off_one, off_two, pairs, state, half, m1, g1m, s1, m2, acc, base):
    def windows(ref, *cols):
        parts = [ref[(pl.ds(at, 3), *cols)] for at in starts]
        return jnp.concatenate(parts, axis=0).reshape(432 * len(starts), ref.shape[-1])

    slabs = []
    for k in range(3):
        down, across = off_one[0, 3 * b + k], off_one[1, 3 * b + k]
        parts = [pairs[pl.ds(SPAN + at + down, 3), pl.ds(SPAN + across, 9)].reshape(432, 384) for at in starts]
        slabs.append(jnp.concatenate(parts, axis=0))
    m = dot(jnp.concatenate(slabs + [s[:, :256] for s in slabs], axis=1), m1[b])
    new = update(windows(state), windows(half), m, g1m.at[b], s1.at[b])
    tiles = packed(new)
    parts = dot(jnp.concatenate(tiles + tiles[:2], axis=1), m2[b])
    for k in range(3):
        down, across = off_two[0, 3 * b + k], off_two[1, 3 * b + k]
        for i, at in enumerate(starts):
            where = (pl.ds(base + at - down, 3), pl.ds(SPAN - across, 9))
            part = parts[432 * i : 432 * i + 432, 256 * k : 256 * k + 192]
            acc[where] = acc[where] + part.reshape(3, 9, 16, C)
    return new.reshape(3 * len(starts), 9, 16, C)


def to_sites(out, value):
    for q in range(4):
        out[:, 9 * q : 9 * q + 9] = value[:, :, 4 * q : 4 * q + 4, :]


def fold(acc, rows):
    for q in range(3):
        low, high = slice(4 * q, 4 * q + 4), slice(4 * q + 4, 4 * q + 8)
        acc[rows, 3:6, high, :] = acc[rows, 3:6, high, :] + acc[rows, 12:15, low, :]
        acc[rows, 9:12, low, :] = acc[rows, 9:12, low, :] + acc[rows, 0:3, high, :]


def outer_kernel(
    off_one, off_two, west, east, mid, west_q, east_q, left_q, right_q, left_g, right_g, m1, g1m, s1, m2,
    left_out, right_out, near, far, pairs, acc,
    side, fresh, whole, sems,
):
    pairs[:, 3:12] = mid[...]
    for at, known, new, sub in ((0, west_q, west, 0), (12, east_q, east, 12)):
        side[...] = known[...]
        side[:, :, sub : sub + 4, :] = new[...]
        tiles = packed(side[...].reshape(720, C))
        for t in range(3):
            pairs[:, at : at + 3, :, 128 * t : 128 * t + 128] = tiles[t].reshape(15, 3, 16, 128)
    acc[...] = jnp.zeros(acc.shape, F32)

    copies = []
    for b, (state, half, out) in enumerate(((left_q, left_g, left_out), (right_q, right_g, right_out))):
        new = block_step(b, (0, 6), off_one, off_two, pairs, state, half, m1, g1m, s1, m2, acc, SPAN)
        to_sites(fresh.at[b], new)
        for i, at in enumerate((0, 6)):
            copies.append(
                pltpu.make_async_copy(fresh.at[b, pl.ds(3 * i, 3)], out.at[pl.ds(at, 3)], sems.at[2 * b + i])
            )
            copies[-1].start()

    for n, at in enumerate((0, 12)):
        rows = slice(at, at + 3)
        fold(acc, rows)
        whole[n, :, 0:3] = acc[rows, 0:3, 0:4, :]
        to_sites(whole.at[n, :, 3:39], acc[rows, 3:12])
        whole[n, :, 39:42] = acc[rows, 12:15, 12:16, :]
    odd = is_odd()
    near[...] = dense(whole[1 - odd])
    far[...] = dense(whole[odd])
    for copy in copies:
        copy.wait()


def outer_rows(off_one, off_two, *operands):
    states = [jax.ShapeDtypeStruct((9, 36, 4, C), F32)] * 2
    smem = pl.BlockSpec(memory_space=pltpu.SMEM)
    return pl.pallas_call(
        outer_kernel,
        out_shape=states
        + results([(3, 63, 4, 128)] * 2)
        + results([(15, 15, 16, 384)], BF16)
        + results([(15, 15, 16, C)]),
        in_specs=[smem, smem] + vmem(13),
        out_specs=[HBM] * 2 + vmem(4),
        scratch_shapes=[
            pltpu.VMEM((15, 3, 16, C), F32),
            pltpu.VMEM((2, 6, 36, 4, C), F32),
            pltpu.VMEM((2, 3, 42, 4, C), F32),
            pltpu.SemaphoreType.DMA((4,)),
        ],
        name="outer_rows",
        compiler_params=params(18),
    )(off_one, off_two, *operands)


def inner_kernel(
    off_one, off_two, left_in, right_in, pairs, acc_in, left_q, right_q, left_g, right_g, m1, g1m, s1, m2,
    left_out, right_out, acc_mid, acc_west, acc_east,
    acc, fresh, sems,
):
    acc[...] = acc_in[3:12]
    copies = []
    for b, (state, half, out) in enumerate(((left_q, left_g, left_out), (right_q, right_g, right_out))):
        new = block_step(b, (3,), off_one, off_two, pairs, state, half, m1, g1m, s1, m2, acc, 0)
        to_sites(fresh.at[b], new)
        copies.append(pltpu.make_async_copy(fresh.at[b], out.at[pl.ds(3, 3)], sems.at[b]))
        copies[b].start()
    fold(acc, slice(0, 9))
    acc_mid[...] = acc[:, 3:12]
    acc_west[...] = acc[:, 0:3, 0:4, :]
    acc_east[...] = acc[:, 12:15, 12:16, :]
    for copy in copies:
        copy.wait()


def inner_rows(off_one, off_two, *operands):
    states = [jax.ShapeDtypeStruct((9, 36, 4, C), F32)] * 2
    smem = pl.BlockSpec(memory_space=pltpu.SMEM)
    return pl.pallas_call(
        inner_kernel,
        out_shape=states + results([(9, 9, 16, C), (9, 3, 4, C), (9, 3, 4, C)]),
        in_specs=[smem, smem, HBM, HBM] + vmem(10),
        out_specs=[HBM] * 2 + vmem(3),
        scratch_shapes=[
            pltpu.VMEM((9, 15, 16, C), F32),
            pltpu.VMEM((2, 3, 36, 4, C), F32),
            pltpu.SemaphoreType.DMA((2,)),
        ],
        input_output_aliases={2: 0, 3: 1},
        name="inner_rows",
        compiler_params=params(14),
    )(off_one, off_two, *operands)


def layer_two_kernel(
    from_top, from_bottom, from_west, from_east, acc_mid, checks_q, checks_g, g2m, s2, out, acc, fresh, sems
):
    acc[...] = acc_mid[...]
    for q in range(4):
        sub = slice(4 * q, 4 * q + 4)
        cols = slice(3 + 9 * q, 12 + 9 * q)
        acc[0:3, :, sub, :] = acc[0:3, :, sub, :] + from_top[:, cols]
        acc[6:9, :, sub, :] = acc[6:9, :, sub, :] + from_bottom[:, cols]
    acc[:, 0:3, 0:4, :] = acc[:, 0:3, 0:4, :] + from_west[...]
    acc[:, 6:9, 12:16, :] = acc[:, 6:9, 12:16, :] + from_east[...]
    new = update(checks_q[...].reshape(1296, C), checks_g[...], acc[...].reshape(1296, C), g2m, s2)
    whole = new.reshape(9, 9, 16, C)
    copies = []
    for g in range(3):
        rows = slice(3 * g, 3 * g + 3)
        to_sites(fresh.at[rows], whole[rows])
        copies.append(pltpu.make_async_copy(fresh.at[rows], out.at[rows], sems.at[g]))
        copies[g].start()
    for copy in copies:
        copy.wait()


def layer_two(from_top, from_bottom, from_west, from_east, *operands):
    return pl.pallas_call(
        layer_two_kernel,
        out_shape=jax.ShapeDtypeStruct((9, 36, 4, C), F32),
        in_specs=vmem(9),
        out_specs=HBM,
        scratch_shapes=[
            pltpu.VMEM((9, 9, 16, C), F32), pltpu.VMEM((9, 36, 4, C), F32), pltpu.SemaphoreType.DMA((3,)),
        ],
        name="layer_two",
        compiler_params=params(12),
    )(from_top, from_bottom, from_west, from_east, *operands)


def exchange(axis, low, high):
    count = lax.axis_size(axis)
    up = [(i, (i + 1) % count) for i in range(count)]
    return lax.ppermute(high, axis, up), lax.ppermute(low, axis, [(b, a) for a, b in up])


def trade(near, far):
    count = lax.axis_size("gx")
    next_chip = [(i, (i + (1 if i % 2 else -1)) % count) for i in range(count)]
    got = lax.ppermute(far, "gx", next_chip)
    return lax.ppermute(near, "gx", [(i, i ^ 1) for i in range(count)]), got


def body(
    check_state, syndrome, left_state, right_state, offsets_one, offsets_two, syndrome_gain,
    mix_one, grow_one, shrink_one, mix_two, grow_two, shrink_two,
):
    site = lambda x: jnp.transpose(x, (1, 2, 0, 3))
    back = lambda x: jnp.transpose(x, (2, 0, 1, 3))
    check, bits, gain = site(check_state), jnp.transpose(syndrome, (1, 0, 2)), syndrome_gain.reshape(1, C)
    near, far, first, last = make_edges(check, bits, gain)
    near, far = trade(near, far)
    middle, m1, g1m, s1, m2, g2h, g2m, s2, left_q, right_q, left_g, right_g = prework(
        check, bits, gain, site(left_state), site(right_state),
        mix_one, grow_one, jnp.swapaxes(shrink_one, 1, 2), mix_two, grow_two, shrink_two.T,
    )
    near, far, middle = lax.optimization_barrier((near, far, middle))
    low, high, top, bottom = make_columns(first, middle, last, near, far)
    west, east = exchange("gy", low, high)
    pairs, west_q, east_q, checks_q, checks_g = make_fields(first, middle, last, top, bottom, g2h)
    steps = (offsets_one.T, offsets_two.T)
    shared = (left_q, right_q, left_g, right_g, m1, g1m, s1, m2)
    left_out, right_out, near, far, pairs, acc = outer_rows(*steps, west, east, pairs, west_q, east_q, *shared)
    near, far = trade(near, far)
    left_out, right_out, acc_mid, acc_west, acc_east = inner_rows(*steps, left_out, right_out, pairs, acc, *shared)
    near, far, acc_mid = lax.optimization_barrier((near, far, acc_mid))
    low, high, from_top, from_bottom = make_sums(acc_west, acc_east, near, far)
    from_west, from_east = exchange("gy", low, high)
    check_out = layer_two(
        from_top, from_bottom, from_west, from_east, acc_mid, checks_q, checks_g, g2m, s2
    )
    return back(left_out), back(right_out), back(check_out)


def solution(mesh):
    site = P(None, "gx", "gy", None)
    in_specs = (site, P(None, "gx", "gy"), site, site) + (P(),) * 9
    return jax.shard_map(body, mesh=mesh, in_specs=in_specs, out_specs=(site,) * 3, check_vma=False)
```

```python
import jax
import jax.numpy as jnp
from jax import lax
from jax.experimental import pallas as pl
from jax.experimental.pallas import tpu as pltpu
from jax.sharding import PartitionSpec as P

SPAN = 3
C = 192
F32 = jnp.float32
BF16 = jnp.bfloat16


def split(x):
    hi = x.astype(BF16)
    lo = (x - hi.astype(F32)).astype(BF16)
    return hi, lo


def packed(x):
    first, rest = x[:, :128], x[:, 128:]
    hi, lo = split(first)
    twice = jnp.concatenate([rest, rest], axis=1)
    rest_hi = twice.astype(BF16).astype(F32)
    lane = lax.broadcasted_iota(jnp.int32, twice.shape, 1)
    both = jnp.where(lane < 64, rest_hi, twice - rest_hi).astype(BF16)
    return [hi, both, lo]


def dot(a, b):
    return lax.dot_general(a, b, (((1,), (0,)), ((), ())), preferred_element_type=F32)


def dot_t(a, b):
    return lax.dot_general(a, b, (((1,), (1,)), ((), ())), preferred_element_type=F32)


def silu(v):
    return 0.5 * v * (1.0 + jnp.tanh(0.5 * v))


def vmem(count):
    return [pl.BlockSpec(memory_space=pltpu.VMEM)] * count


def params(mib):
    return pltpu.CompilerParams(vmem_limit_bytes=mib * 1024 * 1024)


HBM = pl.BlockSpec(memory_space=pltpu.HBM)


def far_off(*arrays):
    return [pltpu.with_memory_space_constraint(x, pltpu.HBM) for x in arrays]


def results(shapes, kind=F32):
    return [jax.ShapeDtypeStruct(shape, kind) for shape in shapes]


def fetch(pairs, sems):
    copies = [pltpu.make_async_copy(src, dst, sems.at[i]) for i, (src, dst) in enumerate(pairs)]
    for copy in copies:
        copy.start()
    return copies


def pair_rows(out, weights):
    hi, lo = split(weights)
    n = weights.shape[1]
    out[0:192, :n] = hi
    out[192:256, :n] = hi[128:192]
    out[256:384, :n] = hi[0:128]
    return lo


def low_rows(out, lo):
    n = lo.shape[1]
    out[0:192, :n] = lo
    out[192:256, :n] = jnp.zeros((64, n), BF16)


def picker():
    column = lax.broadcasted_iota(jnp.int32, (36, 8, 36), 0)
    lane = lax.broadcasted_iota(jnp.int32, (36, 8, 36), 2)
    return (column == lane).astype(F32)


def checks_row(check, syndrome, gain, pick):
    bits = (2 * syndrome - 1).astype(F32)
    bits = jnp.concatenate([bits, bits], axis=0)
    sign = jnp.sum(pick * bits[None], axis=-1, keepdims=True)[:, 0:4, :]
    return check + sign * gain


def is_odd(axis="gx"):
    return lax.rem(lax.axis_index(axis), 2)


def dense(value):
    half = value.shape[1] // 2
    rest = jnp.concatenate([value[:, :half, :, 128:], value[:, half:, :, 128:]], axis=-1)
    return jnp.concatenate([value[:, :, :, :128], rest], axis=1)


def undense(out, ref):
    columns = out.shape[1]
    half = columns // 2
    out[:, :, :, :128] = ref[:, :columns]
    out[:, :half, :, 128:] = ref[:, columns:, :, :64]
    out[:, half:, :, 128:] = ref[:, columns:, :, 64:]


def edges_kernel(check, syndrome, gain, far, near, first, last, rows, bits, gains, sems):
    copies = fetch(
        [(syndrome, bits), (gain, gains)] + [(check.at[r], rows.at[r]) for r in (0, 1, 2, 6, 7, 8)], sems
    )
    pick = picker()
    copies[0].wait()
    copies[1].wait()
    for n, r in enumerate((0, 1, 2, 6, 7, 8)):
        copies[2 + n].wait()
        value = checks_row(rows[r], bits[r], gains[...], pick)
        if r < 3:
            first[r] = value
        else:
            last[r - 6] = value
    odd = is_odd() == 1
    low, high = dense(first[...]), dense(last[...])
    near[...] = jnp.where(odd, low, high)
    far[...] = jnp.where(odd, high, low)


def make_edges(check, syndrome, gain):
    return pl.pallas_call(
        edges_kernel,
        out_shape=results([(3, 54, 4, 128)] * 2 + [(3, 36, 4, C)] * 2),
        in_specs=[HBM] * 3,
        out_specs=vmem(4),
        scratch_shapes=[
            pltpu.VMEM((9, 36, 4, C), F32), pltpu.VMEM((9, 4, 36), jnp.int32), pltpu.VMEM((1, C), F32),
            pltpu.SemaphoreType.DMA((8,)),
        ],
        name="edges",
        compiler_params=params(8),
    )(*far_off(check, syndrome, gain))


def grow(src, out_h, out_m):
    for at, out in ((0, out_h), (192, out_m)):
        low_rows(out.at[384:640], pair_rows(out.at[0:384], src[at : at + 192, :]))


def shrink(src, out):
    hi, lo = split(src[...])
    out[:, 0:384] = hi
    out[:, 384:768] = hi
    out[:, 768:1152] = lo


def prework_kernel(
    check, syndrome, gain, left, right, mix_one, grow_one, shrink_one, mix_two, first, last,
    middle, m1, g1m, s1, m2, left_q, right_q, checks_q, left_g, right_g, center,
    g1h, rows, bits, gains, lefts, rights, mix_1, grow_1, shrink_1, mix_2, sems,
):
    copies = fetch(
        [
            (left, lefts), (grow_one, grow_1), (right, rights), (mix_one, mix_1), (mix_two, mix_2),
            (shrink_one, shrink_1), (syndrome, bits), (gain, gains), (check.at[3:6], rows),
        ],
        sems,
    )

    def mixes(b):
        for k in range(3):
            low = pair_rows(m1.at[b, 384 * k : 384 * k + 384], mix_1[3 * b + k])
            low_rows(m1.at[b, 1152 + 256 * k : 1408 + 256 * k], low)
            out = m2.at[b, :, 256 * k : 256 * k + 256]
            low_rows(out.at[384:640], pair_rows(out.at[0:384], mix_2[3 * b + k]))

    def half(b, ref, quart, out):
        copies[2 * b].wait()
        for q in range(4):
            quart[:, :, 4 * q : 4 * q + 4, :] = ref[:, 9 * q : 9 * q + 9]
        if b == 0:
            copies[1].wait()
        grow(grow_1.at[b], g1h.at[b], g1m.at[b])
        tiles = packed(quart[...].reshape(1296, C))
        yield
        out[...] = dot(jnp.concatenate(tiles + tiles[:2], axis=1), g1h[b]).reshape(9, 9, 16, 384)
        if b == 0:
            for copy in copies[3:6]:
                copy.wait()
        mixes(b)
        shrink(shrink_1.at[b], s1.at[b])
        yield

    def checks():
        yield
        for copy in copies[6:]:
            copy.wait()
        pick = picker()
        for r in range(3):
            middle[r] = checks_row(rows[r], bits[3 + r], gains[...], pick)
        for r, ref in enumerate((first, middle, last)):
            for q in range(4):
                checks_q[3 * r : 3 * r + 3, :, 4 * q : 4 * q + 4, :] = ref[:, 9 * q : 9 * q + 9]
        tiles = packed(checks_q[...].reshape(1296, C))
        for t in range(3):
            center[:, :, :, 128 * t : 128 * t + 128] = tiles[t].reshape(9, 9, 16, 128)

    together(half(0, lefts, left_q, left_g), half(1, rights, right_q, right_g), checks())


def prework(*operands):
    weights = [(2, 1920, C), (2, 640, 384), (2, C, 1152), (2, 640, 768)]
    states = [(9, 9, 16, C)] * 3 + [(9, 9, 16, 384)] * 2
    scratch = [(3, 36, 4, C), (9, 4, 36), (1, C), (9, 36, 4, C), (9, 36, 4, C), (6, C, C), (2, 384, 384)]
    scratch += [(2, C, 384), (6, C, C)]
    return pl.pallas_call(
        prework_kernel,
        out_shape=results([(3, 36, 4, C)])
        + results(weights, BF16)
        + results(states)
        + results([(9, 9, 16, 384)], BF16),
        in_specs=[HBM] * 9 + vmem(2),
        out_specs=vmem(11),
        scratch_shapes=[pltpu.VMEM((2, 640, 384), BF16)]
        + [pltpu.VMEM(s, jnp.int32 if s == (9, 4, 36) else F32) for s in scratch]
        + [pltpu.SemaphoreType.DMA((9,))],
        name="prework",
        compiler_params=params(18),
    )(*far_off(*operands[:9]), *operands[9:])


def columns_kernel(first, middle, last, near, far, to_far, to_near, top, bottom, rows, low, high):
    undense(rows.at[0], near)
    undense(rows.at[1], far)
    odd = is_odd()
    top[...] = rows[1 - odd]
    bottom[...] = rows[odd]
    for r, ref in enumerate((top, first, middle, last, bottom)):
        low[3 * r : 3 * r + 3] = ref[:, 0:3]
        high[3 * r : 3 * r + 3] = ref[:, 33:36]
    odd = is_odd("gy") == 1
    to_far[...] = jnp.where(odd, high[...], low[...])
    to_near[...] = jnp.where(odd, low[...], high[...])


def make_columns(*operands):
    return pl.pallas_call(
        columns_kernel,
        out_shape=results([(15, 3, 4, C)] * 2 + [(3, 36, 4, C)] * 2),
        in_specs=vmem(5),
        out_specs=vmem(4),
        scratch_shapes=[pltpu.VMEM((2, 3, 36, 4, C), F32)] + [pltpu.VMEM((15, 3, 4, C), F32)] * 2,
        name="columns",
        compiler_params=params(6),
    )(*operands)


def sums_kernel(acc_west, acc_east, near, far, to_far, to_near, top, bottom, rows, low, high):
    undense(rows.at[0], near)
    undense(rows.at[1], far)
    odd = is_odd()
    top[...] = rows[1 - odd]
    bottom[...] = rows[odd]
    for ref, acc, cols in ((low, acc_west, slice(0, 3)), (high, acc_east, slice(39, 42))):
        ref[0:3] = acc[0:3] + top[:, cols]
        ref[3:6] = acc[3:6]
        ref[6:9] = acc[6:9] + bottom[:, cols]
    odd = is_odd("gy") == 1
    to_far[...] = jnp.where(odd, high[...], low[...])
    to_near[...] = jnp.where(odd, low[...], high[...])


def make_sums(*operands):
    return pl.pallas_call(
        sums_kernel,
        out_shape=results([(9, 3, 4, C)] * 2 + [(3, 42, 4, C)] * 2),
        in_specs=vmem(4),
        out_specs=vmem(4),
        scratch_shapes=[pltpu.VMEM((2, 3, 42, 4, C), F32)] + [pltpu.VMEM((9, 3, 4, C), F32)] * 2,
        name="sums",
        compiler_params=params(6),
    )(*operands)


def update(h, half, m, grow, shrink):
    mean = jnp.sum(h * h + m * m, axis=-1, keepdims=True) * (1.0 / 384.0)
    mp = packed(m)
    yield
    grown = dot(jnp.concatenate(mp + mp[:2], axis=1), grow[...])
    yield
    hi, lo = split(silu((grown + half) * lax.rsqrt(mean + 1e-05)))
    yield
    yield h + dot_t(jnp.concatenate([hi, lo, hi], axis=1), shrink[...])


def together(*steps):
    last = [None] * len(steps)
    live = list(range(len(steps)))
    while live:
        for i in list(live):
            try:
                last[i] = next(steps[i])
            except StopIteration:
                live.remove(i)
    return last


def block_step(b, pieces, off_one, off_two, pairs, margin, state, half, m1, g1m, s1, m2, acc, base):
    sizes = [48 * wide for _, _, wide in pieces]

    def windows(ref, down=0, across=0):
        parts = [
            ref[pl.ds(row + down, 3), pl.ds(col + across, wide)].reshape(48 * wide, ref.shape[-1])
            for row, col, wide in pieces
        ]
        return jnp.concatenate(parts, axis=0)

    slabs = [
        windows(pairs, SPAN + off_one[0, 3 * b + k], margin + off_one[1, 3 * b + k]) for k in range(3)
    ]
    m = dot(jnp.concatenate(slabs + [s[:, :256] for s in slabs], axis=1), m1[b])
    yield
    for new in update(windows(state), windows(half), m, g1m.at[b], s1.at[b]):
        yield
    tiles = packed(new)
    yield
    parts = dot(jnp.concatenate(tiles + tiles[:2], axis=1), m2[b])
    yield
    for k in range(3):
        down, across = off_two[0, 3 * b + k], off_two[1, 3 * b + k]
        at = 0
        for size, (row, col, wide) in zip(sizes, pieces):
            where = (pl.ds(base + row - down, 3), pl.ds(SPAN + col - across, wide))
            acc[where] = acc[where] + parts[at : at + size, 256 * k : 256 * k + 192].reshape(3, wide, 16, C)
            at += size
    at, news = 0, []
    for size, (row, col, wide) in zip(sizes, pieces):
        news.append(new[at : at + size].reshape(3, wide, 16, C))
        at += size
    yield news


def layer_one_steps(pieces, off_one, off_two, pairs, margin, states, halves, m1, g1m, s1, m2, acc, base):
    return together(
        *(
            block_step(b, pieces, off_one, off_two, pairs, margin, states[b], halves[b], m1, g1m, s1, m2, acc, base)
            for b in range(2)
        )
    )


def to_sites(out, value, col=0):
    for q in range(4):
        out[:, 9 * q + col : 9 * q + col + value.shape[1]] = value[:, :, 4 * q : 4 * q + 4, :]


def fold(acc, rows):
    for q in range(3):
        low, high = slice(4 * q, 4 * q + 4), slice(4 * q + 4, 4 * q + 8)
        acc[rows, 3:6, high, :] = acc[rows, 3:6, high, :] + acc[rows, 12:15, low, :]
        acc[rows, 9:12, low, :] = acc[rows, 9:12, low, :] + acc[rows, 0:3, high, :]


def core_kernel(
    off_one, off_two, first, middle, last, top, bottom, center, left_q, right_q, left_g, right_g, m1, g1m, s1, m2,
    mid, west_q, east_q, acc, left_core, right_core,
    field,
):
    mid[3:12] = center[...]
    for at, ref in ((0, top), (12, bottom)):
        for q in range(4):
            field[:, :, 4 * q : 4 * q + 4, :] = ref[:, 9 * q : 9 * q + 9]
        tiles = packed(field[...].reshape(432, C))
        for t in range(3):
            mid[at : at + 3, :, :, 128 * t : 128 * t + 128] = tiles[t].reshape(3, 9, 16, 128)
    for r, ref in enumerate((top, first, middle, last, bottom)):
        for q in range(3):
            east_q[3 * r : 3 * r + 3, :, 4 * q : 4 * q + 4, :] = ref[:, 9 * q + 9 : 9 * q + 12]
            west_q[3 * r : 3 * r + 3, :, 4 * q + 4 : 4 * q + 8, :] = ref[:, 9 * q + 6 : 9 * q + 9]
    acc[...] = jnp.zeros(acc.shape, F32)
    news = layer_one_steps(
        [(0, 3, 3), (6, 3, 3)], off_one, off_two, mid, 0, (left_q, right_q), (left_g, right_g), m1, g1m, s1, m2, acc,
        SPAN,
    )
    for ref, (low, high) in zip((left_core, right_core), news):
        ref[0:3] = low
        ref[3:6] = high


def core_columns(off_one, off_two, *operands):
    smem = pl.BlockSpec(memory_space=pltpu.SMEM)
    shapes = [(15, 3, 16, C), (15, 3, 16, C), (15, 15, 16, C), (6, 3, 16, C), (6, 3, 16, C)]
    return pl.pallas_call(
        core_kernel,
        out_shape=results([(15, 9, 16, 384)], BF16) + results(shapes),
        in_specs=[smem, smem] + vmem(14),
        out_specs=vmem(6),
        scratch_shapes=[pltpu.VMEM((3, 9, 16, C), F32)],
        name="core_columns",
        compiler_params=params(12),
    )(off_one, off_two, *operands)


def outer_kernel(
    off_one, off_two, near_in, far_in, mid, west_q, east_q, acc_core, left_core, right_core,
    left_q, right_q, left_g, right_g, m1, g1m, s1, m2,
    left_out, right_out, far, near, pairs, acc,
    side, fresh, whole, sems,
):
    pairs[:, 3:12] = mid[...]
    odd = is_odd("gy") == 1
    west = jnp.where(odd, near_in[...], far_in[...])
    east = jnp.where(odd, far_in[...], near_in[...])
    for at, known, new, sub in ((0, west_q, west, 0), (12, east_q, east, 12)):
        side[...] = known[...]
        side[:, :, sub : sub + 4, :] = new
        tiles = packed(side[...].reshape(720, C))
        for t in range(3):
            pairs[:, at : at + 3, :, 128 * t : 128 * t + 128] = tiles[t].reshape(15, 3, 16, 128)
    acc[...] = acc_core[...]
    pieces = [(0, 0, 3), (0, 6, 3), (6, 0, 3), (6, 6, 3)]
    news = layer_one_steps(
        pieces, off_one, off_two, pairs, SPAN, (left_q, right_q), (left_g, right_g), m1, g1m, s1, m2, acc, SPAN
    )
    copies = []
    for b, (new, core, out) in enumerate(zip(news, (left_core, right_core), (left_out, right_out))):
        to_sites(fresh.at[b], core[...], 3)
        for (row, col, _), value in zip(pieces, new):
            to_sites(fresh.at[b, row // 2 : row // 2 + 3], value, col)
        for i, at in enumerate((0, 6)):
            copies.append(
                pltpu.make_async_copy(fresh.at[b, pl.ds(3 * i, 3)], out.at[pl.ds(at, 3)], sems.at[2 * b + i])
            )
            copies[-1].start()

    for n, at in enumerate((0, 12)):
        rows = slice(at, at + 3)
        fold(acc, rows)
        whole[n, :, 0:3] = acc[rows, 0:3, 0:4, :]
        to_sites(whole.at[n, :, 3:39], acc[rows, 3:12])
        whole[n, :, 39:42] = acc[rows, 12:15, 12:16, :]
    odd = is_odd()
    near[...] = dense(whole[1 - odd])
    far[...] = dense(whole[odd])
    for copy in copies:
        copy.wait()


def outer_rows(off_one, off_two, *operands):
    states = [jax.ShapeDtypeStruct((9, 36, 4, C), F32)] * 2
    smem = pl.BlockSpec(memory_space=pltpu.SMEM)
    return pl.pallas_call(
        outer_kernel,
        out_shape=states
        + results([(3, 63, 4, 128)] * 2)
        + results([(15, 15, 16, 384)], BF16)
        + results([(15, 15, 16, C)]),
        in_specs=[smem, smem] + vmem(16),
        out_specs=[HBM] * 2 + vmem(4),
        scratch_shapes=[
            pltpu.VMEM((15, 3, 16, C), F32),
            pltpu.VMEM((2, 6, 36, 4, C), F32),
            pltpu.VMEM((2, 3, 42, 4, C), F32),
            pltpu.SemaphoreType.DMA((4,)),
        ],
        name="outer_rows",
        compiler_params=params(18),
    )(off_one, off_two, *operands)


def inner_kernel(
    off_one, off_two, left_in, right_in, grow_two, shrink_two, pairs, acc_in, center,
    left_q, right_q, left_g, right_g, m1, g1m, s1, m2,
    left_out, right_out, acc_mid, acc_west, acc_east, checks_g, g2m, s2,
    acc, fresh, grow_2, shrink_2, g2h, sems,
):
    loads = [
        pltpu.make_async_copy(src, dst, sems.at[2 + i])
        for i, (src, dst) in enumerate(((grow_two, grow_2), (shrink_two, shrink_2)))
    ]
    for copy in loads:
        copy.start()
    acc[...] = acc_in[3:12]
    copies = []
    news = layer_one_steps(
        [(3, 0, 9)], off_one, off_two, pairs, SPAN, (left_q, right_q), (left_g, right_g), m1, g1m, s1, m2, acc, 0
    )
    for b, ((new,), out) in enumerate(zip(news, (left_out, right_out))):
        to_sites(fresh.at[b], new)
        copies.append(pltpu.make_async_copy(fresh.at[b], out.at[pl.ds(3, 3)], sems.at[b]))
        copies[b].start()
    for copy in loads:
        copy.wait()
    grow(grow_2, g2h, g2m)
    shrink(shrink_2, s2)
    tiles = center[...].reshape(1296, 384)
    checks_g[...] = dot(jnp.concatenate([tiles, tiles[:, :256]], axis=1), g2h[...]).reshape(9, 9, 16, 384)
    fold(acc, slice(0, 9))
    acc_mid[...] = acc[:, 3:12]
    acc_west[...] = acc[:, 0:3, 0:4, :]
    acc_east[...] = acc[:, 12:15, 12:16, :]
    for copy in copies:
        copy.wait()


def inner_rows(off_one, off_two, left_out, right_out, grow_two, shrink_two, *operands):
    states = [jax.ShapeDtypeStruct((9, 36, 4, C), F32)] * 2
    smem = pl.BlockSpec(memory_space=pltpu.SMEM)
    return pl.pallas_call(
        inner_kernel,
        out_shape=states
        + results([(9, 9, 16, C), (9, 3, 4, C), (9, 3, 4, C), (9, 9, 16, 384)])
        + results([(640, 384), (C, 1152)], BF16),
        in_specs=[smem, smem] + [HBM] * 4 + vmem(11),
        out_specs=[HBM] * 2 + vmem(6),
        scratch_shapes=[
            pltpu.VMEM((9, 15, 16, C), F32),
            pltpu.VMEM((2, 3, 36, 4, C), F32),
            pltpu.VMEM((384, 384), F32),
            pltpu.VMEM((C, 384), F32),
            pltpu.VMEM((640, 384), BF16),
            pltpu.SemaphoreType.DMA((4,)),
        ],
        input_output_aliases={2: 0, 3: 1},
        name="inner_rows",
        compiler_params=params(16),
    )(off_one, off_two, left_out, right_out, *far_off(grow_two, shrink_two), *operands)


def all_columns_kernel(
    from_top, from_bottom, acc_mid, checks_q, checks_g, g2m, s2, out, edge_m, edge_h, edge_g, acc, fresh, sems
):
    acc[...] = acc_mid[...]
    for q in range(4):
        sub = slice(4 * q, 4 * q + 4)
        cols = slice(3 + 9 * q, 12 + 9 * q)
        acc[0:3, :, sub, :] = acc[0:3, :, sub, :] + from_top[:, cols]
        acc[6:9, :, sub, :] = acc[6:9, :, sub, :] + from_bottom[:, cols]
    for edge, whole in ((edge_m, acc), (edge_h, checks_q), (edge_g, checks_g)):
        edge[:, :, 0:4, :] = whole[:, 0:3, 0:4, :]
        edge[:, :, 4:8, :] = whole[:, 6:9, 12:16, :]
    groups = (slice(0, 5), slice(5, 9))
    news = together(
        *(
            update(checks_q[r].reshape(-1, C), checks_g[r].reshape(-1, 384), acc[r].reshape(-1, C), g2m, s2)
            for r in groups
        )
    )
    copies = []
    for g, (rows, new) in enumerate(zip(groups, news)):
        to_sites(fresh.at[rows], new.reshape(-1, 9, 16, C))
        copies.append(pltpu.make_async_copy(fresh.at[rows], out.at[rows], sems.at[g]))
        copies[g].start()
    for copy in copies:
        copy.wait()


def all_columns(*operands):
    return pl.pallas_call(
        all_columns_kernel,
        out_shape=[jax.ShapeDtypeStruct((9, 36, 4, C), F32)]
        + results([(9, 3, 8, C), (9, 3, 8, C), (9, 3, 8, 384)]),
        in_specs=vmem(7),
        out_specs=[HBM] + vmem(3),
        scratch_shapes=[
            pltpu.VMEM((9, 9, 16, C), F32), pltpu.VMEM((9, 36, 4, C), F32), pltpu.SemaphoreType.DMA((2,)),
        ],
        name="all_columns",
        compiler_params=params(14),
    )(*operands)


def edge_columns_kernel(out_in, near, far, edge_m, edge_h, edge_g, g2m, s2, out, message, fresh, sems):
    message[...] = edge_m[...]
    odd = is_odd("gy") == 1
    message[:, :, 0:4, :] = message[:, :, 0:4, :] + jnp.where(odd, near[...], far[...])
    message[:, :, 4:8, :] = message[:, :, 4:8, :] + jnp.where(odd, far[...], near[...])
    (new,) = together(
        update(edge_h[...].reshape(216, C), edge_g[...].reshape(216, 384), message[...].reshape(216, C), g2m, s2)
    )
    new = new.reshape(9, 3, 8, C)
    copies = []
    for n, at in enumerate((0, 33)):
        fresh[n] = new[:, :, 4 * n : 4 * n + 4, :]
        copies.append(pltpu.make_async_copy(fresh.at[n], out.at[:, pl.ds(at, 3)], sems.at[n]))
        copies[n].start()
    for copy in copies:
        copy.wait()


def edge_columns(*operands):
    return pl.pallas_call(
        edge_columns_kernel,
        out_shape=jax.ShapeDtypeStruct((9, 36, 4, C), F32),
        in_specs=[HBM] + vmem(7),
        out_specs=HBM,
        scratch_shapes=[
            pltpu.VMEM((9, 3, 8, C), F32), pltpu.VMEM((2, 9, 3, 4, C), F32), pltpu.SemaphoreType.DMA((2,)),
        ],
        input_output_aliases={0: 0},
        name="edge_columns",
        compiler_params=params(8),
    )(*operands)


def trade(near, far, axis):
    count = lax.axis_size(axis)
    beyond = [(i, (i + (1 if i % 2 else -1)) % count) for i in range(count)]
    got = lax.ppermute(far, axis, beyond)
    return lax.ppermute(near, axis, [(i, i ^ 1) for i in range(count)]), got


def body(
    check_state, syndrome, left_state, right_state, offsets_one, offsets_two, syndrome_gain,
    mix_one, grow_one, shrink_one, mix_two, grow_two, shrink_two,
):
    site = lambda x: jnp.transpose(x, (1, 2, 0, 3))
    back = lambda x: jnp.transpose(x, (2, 0, 1, 3))
    check, bits, gain = site(check_state), jnp.transpose(syndrome, (1, 0, 2)), syndrome_gain.reshape(1, C)
    far, near, first, last = make_edges(check, bits, gain)
    near, far = trade(near, far, "gx")
    middle, m1, g1m, s1, m2, left_q, right_q, checks_q, left_g, right_g, center = prework(
        check, bits, gain, site(left_state), site(right_state),
        mix_one, grow_one, jnp.swapaxes(shrink_one, 1, 2), mix_two, first, last,
    )
    near, far, middle = lax.optimization_barrier((near, far, middle))
    far, near, top, bottom = make_columns(first, middle, last, near, far)
    near, far = trade(near, far, "gy")
    steps = (offsets_one.T, offsets_two.T)
    shared = (left_q, right_q, left_g, right_g, m1, g1m, s1, m2)
    core = core_columns(*steps, first, middle, last, top, bottom, center, *shared)
    left_out, right_out, far, near, pairs, acc = outer_rows(*steps, near, far, *core, *shared)
    near, far = trade(near, far, "gx")
    left_out, right_out, acc_mid, acc_west, acc_east, checks_g, g2m, s2 = inner_rows(
        *steps, left_out, right_out, grow_two, shrink_two.T, pairs, acc, center, *shared
    )
    near, far, acc_mid = lax.optimization_barrier((near, far, acc_mid))
    far, near, from_top, from_bottom = make_sums(acc_west, acc_east, near, far)
    near, far = trade(near, far, "gy")
    check_out, edge_m, edge_h, edge_g = all_columns(from_top, from_bottom, acc_mid, checks_q, checks_g, g2m, s2)
    check_out = edge_columns(check_out, near, far, edge_m, edge_h, edge_g, g2m, s2)
    return back(left_out), back(right_out), back(check_out)


def solution(mesh):
    site = P(None, "gx", "gy", None)
    in_specs = (site, P(None, "gx", "gy"), site, site) + (P(),) * 9
    return jax.shard_map(body, mesh=mesh, in_specs=in_specs, out_specs=(site,) * 3, check_vma=False)
```

```python
import jax
import jax.numpy as jnp
from jax import lax
from jax.experimental import pallas as pl
from jax.experimental.pallas import tpu as pltpu
from jax.sharding import PartitionSpec as P

SPAN = 3
C = 192
F32 = jnp.float32
BF16 = jnp.bfloat16


def split(x):
    hi = x.astype(BF16)
    lo = (x - hi.astype(F32)).astype(BF16)
    return hi, lo


def packed(x):
    first, rest = x[:, :128], x[:, 128:]
    hi, lo = split(first)
    twice = jnp.concatenate([rest, rest], axis=1)
    rest_hi = twice.astype(BF16).astype(F32)
    lane = lax.broadcasted_iota(jnp.int32, twice.shape, 1)
    both = jnp.where(lane < 64, rest_hi, twice - rest_hi).astype(BF16)
    return [hi, both, lo]


def dot(a, b):
    return lax.dot_general(a, b, (((1,), (0,)), ((), ())), preferred_element_type=F32)


def dot_t(a, b):
    return lax.dot_general(a, b, (((1,), (1,)), ((), ())), preferred_element_type=F32)


def silu(v):
    return 0.5 * v * (1.0 + jnp.tanh(0.5 * v))


def vmem(count):
    return [pl.BlockSpec(memory_space=pltpu.VMEM)] * count


def params(mib):
    return pltpu.CompilerParams(vmem_limit_bytes=mib * 1024 * 1024)


HBM = pl.BlockSpec(memory_space=pltpu.HBM)


def far_off(*arrays):
    return [pltpu.with_memory_space_constraint(x, pltpu.HBM) for x in arrays]


def results(shapes, kind=F32):
    return [jax.ShapeDtypeStruct(shape, kind) for shape in shapes]


def fetch(pairs, sems):
    copies = [pltpu.make_async_copy(src, dst, sems.at[i]) for i, (src, dst) in enumerate(pairs)]
    for copy in copies:
        copy.start()
    return copies


def pair_rows(out, weights):
    hi, lo = split(weights)
    n = weights.shape[1]
    out[0:192, :n] = hi
    out[192:256, :n] = hi[128:192]
    out[256:384, :n] = hi[0:128]
    return lo


def low_rows(out, lo):
    n = lo.shape[1]
    out[0:192, :n] = lo
    out[192:256, :n] = jnp.zeros((64, n), BF16)


def picker():
    column = lax.broadcasted_iota(jnp.int32, (36, 8, 36), 0)
    lane = lax.broadcasted_iota(jnp.int32, (36, 8, 36), 2)
    return (column == lane).astype(F32)


def gains_row(syndrome, gain, pick):
    bits = (2 * syndrome - 1).astype(F32)
    bits = jnp.concatenate([bits, bits], axis=0)
    sign = jnp.sum(pick * bits[None], axis=-1, keepdims=True)[:, 0:4, :]
    return sign * gain


def is_odd(axis="gx"):
    return lax.rem(lax.axis_index(axis), 2)


def dense(value):
    half = value.shape[1] // 2
    rest = jnp.concatenate([value[:, :half, :, 128:], value[:, half:, :, 128:]], axis=-1)
    return jnp.concatenate([value[:, :, :, :128], rest], axis=1)


def undense(out, ref):
    columns = out.shape[1]
    half = columns // 2
    out[:, :, :, :128] = ref[:, :columns]
    out[:, :half, :, 128:] = ref[:, columns:, :, :64]
    out[:, half:, :, 128:] = ref[:, columns:, :, 64:]


def edges_kernel(check, syndrome, gain, far, near, first, last, rows, bits, gains, sems):
    copies = fetch(
        [(syndrome, bits), (gain, gains)] + [(check.at[pl.ds(r, 3)], rows.at[pl.ds(r, 3)]) for r in (0, 6)], sems
    )
    pick = picker()
    copies[0].wait()
    copies[1].wait()
    for r in range(3):
        first[r] = gains_row(bits[r], gains[...], pick)
        last[r] = gains_row(bits[6 + r], gains[...], pick)
    copies[2].wait()
    first[...] = first[...] + rows[0:3]
    copies[3].wait()
    last[...] = last[...] + rows[6:9]
    odd = is_odd() == 1
    low, high = dense(first[...]), dense(last[...])
    near[...] = jnp.where(odd, low, high)
    far[...] = jnp.where(odd, high, low)


def make_edges(check, syndrome, gain):
    return pl.pallas_call(
        edges_kernel,
        out_shape=results([(3, 54, 4, 128)] * 2 + [(3, 36, 4, C)] * 2),
        in_specs=[HBM] * 3,
        out_specs=vmem(4),
        scratch_shapes=[
            pltpu.VMEM((9, 36, 4, C), F32), pltpu.VMEM((9, 4, 36), jnp.int32), pltpu.VMEM((1, C), F32),
            pltpu.SemaphoreType.DMA((4,)),
        ],
        name="edges",
        compiler_params=params(8),
    )(*far_off(check, syndrome, gain))


def grow(src, out_h, out_m):
    for at, out in ((0, out_h), (192, out_m)):
        low_rows(out.at[384:640], pair_rows(out.at[0:384], src[at : at + 192, :]))


def shrink(src, out):
    hi, lo = split(src[...])
    out[:, 0:384] = hi
    out[:, 384:768] = hi
    out[:, 768:1152] = lo


def prework_kernel(
    check, syndrome, gain, left, right, mix_one, grow_one, shrink_one, mix_two, first, last,
    middle, m1, g1m, s1, m2, left_q, right_q, checks_q, left_g, right_g, pairs, acc,
    g1h, rows, bits, gains, lefts, rights, mix_1, grow_1, shrink_1, mix_2, sems,
):
    copies = fetch(
        [
            (left, lefts), (grow_one, grow_1), (right, rights), (mix_one, mix_1), (mix_two, mix_2),
            (shrink_one, shrink_1), (syndrome, bits), (gain, gains), (check.at[3:6], rows),
        ],
        sems,
    )

    def mixes(b):
        for k in range(3):
            low = pair_rows(m1.at[b, 384 * k : 384 * k + 384], mix_1[3 * b + k])
            low_rows(m1.at[b, 1152 + 256 * k : 1408 + 256 * k], low)
            out = m2.at[b, :, 256 * k : 256 * k + 256]
            low_rows(out.at[384:640], pair_rows(out.at[0:384], mix_2[3 * b + k]))

    def half(b, ref, quart, out):
        copies[2 * b].wait()
        for q in range(4):
            quart[:, :, 4 * q : 4 * q + 4, :] = ref[:, 9 * q : 9 * q + 9]
        if b == 0:
            copies[1].wait()
        grow(grow_1.at[b], g1h.at[b], g1m.at[b])
        tiles = packed(quart[...].reshape(1296, C))
        yield
        out[...] = dot(jnp.concatenate(tiles + tiles[:2], axis=1), g1h[b]).reshape(9, 9, 16, 384)
        if b == 0:
            for copy in copies[3:6]:
                copy.wait()
        mixes(b)
        shrink(shrink_1.at[b], s1.at[b])
        yield

    def checks():
        yield
        for copy in copies[6:]:
            copy.wait()
        pick = picker()
        for r in range(3):
            middle[r] = rows[r] + gains_row(bits[3 + r], gains[...], pick)
        for r, ref in enumerate((first, middle, last)):
            for q in range(4):
                checks_q[3 * r : 3 * r + 3, :, 4 * q : 4 * q + 4, :] = ref[:, 9 * q : 9 * q + 9]
        tiles = packed(checks_q[...].reshape(1296, C))
        for t in range(3):
            pairs[3:12, 3:12, :, 128 * t : 128 * t + 128] = tiles[t].reshape(9, 9, 16, 128)
        acc[...] = jnp.zeros(acc.shape, F32)

    together(half(0, lefts, left_q, left_g), half(1, rights, right_q, right_g), checks())


def prework(*operands):
    weights = [(2, 1920, C), (2, 640, 384), (2, C, 1152), (2, 640, 768)]
    states = [(9, 9, 16, C)] * 3 + [(9, 9, 16, 384)] * 2
    scratch = [(3, 36, 4, C), (9, 4, 36), (1, C), (9, 36, 4, C), (9, 36, 4, C), (6, C, C), (2, 384, 384)]
    scratch += [(2, C, 384), (6, C, C)]
    return pl.pallas_call(
        prework_kernel,
        out_shape=results([(3, 36, 4, C)])
        + results(weights, BF16)
        + results(states)
        + results([(15, 15, 16, 384)], BF16)
        + results([(15, 15, 16, C)]),
        in_specs=[HBM] * 9 + vmem(2),
        out_specs=vmem(12),
        scratch_shapes=[pltpu.VMEM((2, 640, 384), BF16)]
        + [pltpu.VMEM(s, jnp.int32 if s == (9, 4, 36) else F32) for s in scratch]
        + [pltpu.SemaphoreType.DMA((9,))],
        name="prework",
        compiler_params=params(18),
    )(*far_off(*operands[:9]), *operands[9:])


def columns_kernel(near, far, first, middle, last, to_far, to_near, top, bottom, rows, low, high):
    undense(rows.at[0], near)
    undense(rows.at[1], far)
    odd = is_odd()
    top[...] = rows[1 - odd]
    bottom[...] = rows[odd]
    for r, ref in enumerate((top, first, middle, last, bottom)):
        low[3 * r : 3 * r + 3] = ref[:, 0:3]
        high[3 * r : 3 * r + 3] = ref[:, 33:36]
    odd = is_odd("gy") == 1
    to_far[...] = jnp.where(odd, high[...], low[...])
    to_near[...] = jnp.where(odd, low[...], high[...])


def make_columns(*operands):
    return pl.pallas_call(
        columns_kernel,
        out_shape=results([(15, 3, 4, C)] * 2 + [(3, 36, 4, C)] * 2),
        in_specs=vmem(5),
        out_specs=vmem(4),
        scratch_shapes=[pltpu.VMEM((2, 3, 36, 4, C), F32)] + [pltpu.VMEM((15, 3, 4, C), F32)] * 2,
        name="columns",
        compiler_params=params(6),
    )(*operands)


def sums_kernel(near, far, acc_west, acc_east, to_far, to_near, top, bottom, rows, low, high):
    undense(rows.at[0], near)
    undense(rows.at[1], far)
    odd = is_odd()
    top[...] = rows[1 - odd]
    bottom[...] = rows[odd]
    for ref, acc, cols in ((low, acc_west, slice(0, 3)), (high, acc_east, slice(39, 42))):
        ref[0:3] = acc[0:3] + top[:, cols]
        ref[3:6] = acc[3:6]
        ref[6:9] = acc[6:9] + bottom[:, cols]
    odd = is_odd("gy") == 1
    to_far[...] = jnp.where(odd, high[...], low[...])
    to_near[...] = jnp.where(odd, low[...], high[...])


def make_sums(*operands):
    return pl.pallas_call(
        sums_kernel,
        out_shape=results([(9, 3, 4, C)] * 2 + [(3, 42, 4, C)] * 2),
        in_specs=vmem(4),
        out_specs=vmem(4),
        scratch_shapes=[pltpu.VMEM((2, 3, 42, 4, C), F32)] + [pltpu.VMEM((9, 3, 4, C), F32)] * 2,
        name="sums",
        compiler_params=params(6),
    )(*operands)


def update(h, half, m, grow, shrink):
    mean = jnp.sum(h * h + m * m, axis=-1, keepdims=True) * (1.0 / 384.0)
    mp = packed(m)
    yield
    grown = dot(jnp.concatenate(mp + mp[:2], axis=1), grow[...])
    yield
    hi, lo = split(silu((grown + half) * lax.rsqrt(mean + 1e-05)))
    yield
    yield h + dot_t(jnp.concatenate([hi, lo, hi], axis=1), shrink[...])


def together(*steps):
    last = [None] * len(steps)
    live = list(range(len(steps)))
    while live:
        for i in list(live):
            try:
                last[i] = next(steps[i])
            except StopIteration:
                live.remove(i)
    return last


def block_step(b, pieces, off_one, off_two, pairs, margin, state, half, m1, g1m, s1, m2, acc, base):
    sizes = [48 * wide for _, _, wide in pieces]

    def windows(ref, down=0, across=0):
        parts = [
            ref[pl.ds(row + down, 3), pl.ds(col + across, wide)].reshape(48 * wide, ref.shape[-1])
            for row, col, wide in pieces
        ]
        return jnp.concatenate(parts, axis=0)

    slabs = [
        windows(pairs, SPAN + off_one[0, 3 * b + k], margin + off_one[1, 3 * b + k]) for k in range(3)
    ]
    m = dot(jnp.concatenate(slabs + [s[:, :256] for s in slabs], axis=1), m1[b])
    yield
    for new in update(windows(state), windows(half), m, g1m.at[b], s1.at[b]):
        yield
    tiles = packed(new)
    yield
    parts = dot(jnp.concatenate(tiles + tiles[:2], axis=1), m2[b])
    yield
    for k in range(3):
        down, across = off_two[0, 3 * b + k], off_two[1, 3 * b + k]
        at = 0
        for size, (row, col, wide) in zip(sizes, pieces):
            where = (pl.ds(base + row - down, 3), pl.ds(SPAN + col - across, wide))
            acc[where] = acc[where] + parts[at : at + size, 256 * k : 256 * k + 192].reshape(3, wide, 16, C)
            at += size
    at, news = 0, []
    for size, (row, col, wide) in zip(sizes, pieces):
        news.append(new[at : at + size].reshape(3, wide, 16, C))
        at += size
    yield news


def layer_one_steps(pieces, off_one, off_two, pairs, margin, states, halves, m1, g1m, s1, m2, acc, base):
    return together(
        *(
            block_step(b, pieces, off_one, off_two, pairs, margin, states[b], halves[b], m1, g1m, s1, m2, acc, base)
            for b in range(2)
        )
    )


def to_sites(out, value, col=0):
    for q in range(4):
        out[:, 9 * q + col : 9 * q + col + value.shape[1]] = value[:, :, 4 * q : 4 * q + 4, :]


def fold(acc, rows):
    for q in range(3):
        low, high = slice(4 * q, 4 * q + 4), slice(4 * q + 4, 4 * q + 8)
        acc[rows, 3:6, high, :] = acc[rows, 3:6, high, :] + acc[rows, 12:15, low, :]
        acc[rows, 9:12, low, :] = acc[rows, 9:12, low, :] + acc[rows, 0:3, high, :]


def core_kernel(
    off_one, off_two, pairs_in, acc_in, first, middle, last, top, bottom, left_q, right_q, left_g, right_g,
    m1, g1m, s1, m2,
    pairs, acc, west_q, east_q, left_core, right_core,
    field,
):
    for at, ref in ((0, top), (12, bottom)):
        for q in range(4):
            field[:, :, 4 * q : 4 * q + 4, :] = ref[:, 9 * q : 9 * q + 9]
        tiles = packed(field[...].reshape(432, C))
        for t in range(3):
            pairs[at : at + 3, 3:12, :, 128 * t : 128 * t + 128] = tiles[t].reshape(3, 9, 16, 128)
    for r, ref in enumerate((top, first, middle, last, bottom)):
        for q in range(3):
            east_q[3 * r : 3 * r + 3, :, 4 * q : 4 * q + 4, :] = ref[:, 9 * q + 9 : 9 * q + 12]
            west_q[3 * r : 3 * r + 3, :, 4 * q + 4 : 4 * q + 8, :] = ref[:, 9 * q + 6 : 9 * q + 9]
    news = layer_one_steps(
        [(0, 3, 3), (6, 3, 3)], off_one, off_two, pairs, SPAN, (left_q, right_q), (left_g, right_g), m1, g1m, s1, m2,
        acc, SPAN,
    )
    for ref, (low, high) in zip((left_core, right_core), news):
        ref[0:3] = low
        ref[3:6] = high


IN_PLACE = [(15, 15, 16, 384), (15, 15, 16, C)]


def core_columns(off_one, off_two, *operands):
    smem = pl.BlockSpec(memory_space=pltpu.SMEM)
    shapes = [(15, 3, 16, C), (15, 3, 16, C), (6, 3, 16, C), (6, 3, 16, C)]
    return pl.pallas_call(
        core_kernel,
        out_shape=results(IN_PLACE[:1], BF16) + results(IN_PLACE[1:] + shapes),
        in_specs=[smem, smem] + vmem(15),
        out_specs=vmem(6),
        scratch_shapes=[pltpu.VMEM((3, 9, 16, C), F32)],
        input_output_aliases={2: 0, 3: 1},
        name="core_columns",
        compiler_params=params(12),
    )(off_one, off_two, *operands)


def outer_kernel(
    off_one, off_two, pairs_in, acc_in, far_in, near_in, west_q, east_q, left_core, right_core,
    left_q, right_q, left_g, right_g, m1, g1m, s1, m2,
    pairs, acc, far, near, fresh,
    side, whole,
):
    odd = is_odd("gy") == 1
    west = jnp.where(odd, near_in[...], far_in[...])
    east = jnp.where(odd, far_in[...], near_in[...])
    for at, known, new, sub in ((0, west_q, west, 0), (12, east_q, east, 12)):
        side[...] = known[...]
        side[:, :, sub : sub + 4, :] = new
        tiles = packed(side[...].reshape(720, C))
        for t in range(3):
            pairs[:, at : at + 3, :, 128 * t : 128 * t + 128] = tiles[t].reshape(15, 3, 16, 128)
    pieces = [(0, 0, 3), (0, 6, 3), (6, 0, 3), (6, 6, 3)]
    news = layer_one_steps(
        pieces, off_one, off_two, pairs, SPAN, (left_q, right_q), (left_g, right_g), m1, g1m, s1, m2, acc, SPAN
    )
    for b, (new, core) in enumerate(zip(news, (left_core, right_core))):
        to_sites(fresh.at[b], core[...], 3)
        for (row, col, _), value in zip(pieces, new):
            to_sites(fresh.at[b, row // 2 : row // 2 + 3], value, col)
    for n, at in enumerate((0, 12)):
        rows = slice(at, at + 3)
        fold(acc, rows)
        whole[n, :, 0:3] = acc[rows, 0:3, 0:4, :]
        to_sites(whole.at[n, :, 3:39], acc[rows, 3:12])
        whole[n, :, 39:42] = acc[rows, 12:15, 12:16, :]
    odd = is_odd()
    near[...] = dense(whole[1 - odd])
    far[...] = dense(whole[odd])


def outer_rows(off_one, off_two, *operands):
    smem = pl.BlockSpec(memory_space=pltpu.SMEM)
    shapes = [(3, 63, 4, 128), (3, 63, 4, 128), (2, 6, 36, 4, C)]
    return pl.pallas_call(
        outer_kernel,
        out_shape=results(IN_PLACE[:1], BF16) + results(IN_PLACE[1:] + shapes),
        in_specs=[smem, smem] + vmem(16),
        out_specs=vmem(5),
        scratch_shapes=[pltpu.VMEM((15, 3, 16, C), F32), pltpu.VMEM((2, 3, 42, 4, C), F32)],
        input_output_aliases={2: 0, 3: 1},
        name="outer_rows",
        compiler_params=params(14),
    )(off_one, off_two, *operands)


def inner_kernel(
    off_one, off_two, grow_two, shrink_two, pairs, acc_in, outer_states,
    left_q, right_q, left_g, right_g, m1, g1m, s1, m2,
    left_out, right_out, acc_mid, acc_west, acc_east, checks_g, g2m, s2,
    acc, fresh, grow_2, shrink_2, g2h, sems,
):
    loads = fetch([(grow_two, grow_2), (shrink_two, shrink_2)], sems)
    copies = [
        pltpu.make_async_copy(outer_states.at[b, pl.ds(at // 2, 3)], out.at[pl.ds(at, 3)], sems.at[2 + 3 * b + n])
        for b, out in enumerate((left_out, right_out))
        for n, at in enumerate((0, 6))
    ]
    for copy in copies:
        copy.start()
    acc[...] = acc_in[3:12]
    news = layer_one_steps(
        [(3, 0, 9)], off_one, off_two, pairs, SPAN, (left_q, right_q), (left_g, right_g), m1, g1m, s1, m2, acc, 0
    )
    for b, ((new,), out) in enumerate(zip(news, (left_out, right_out))):
        to_sites(fresh.at[b], new)
        copies.append(pltpu.make_async_copy(fresh.at[b], out.at[pl.ds(3, 3)], sems.at[4 + 3 * b]))
        copies[-1].start()
    for copy in loads:
        copy.wait()
    grow(grow_2, g2h, g2m)
    shrink(shrink_2, s2)
    tiles = pairs[3:12, 3:12].reshape(1296, 384)
    checks_g[...] = dot(jnp.concatenate([tiles, tiles[:, :256]], axis=1), g2h[...]).reshape(9, 9, 16, 384)
    fold(acc, slice(0, 9))
    acc_mid[...] = acc[:, 3:12]
    acc_west[...] = acc[:, 0:3, 0:4, :]
    acc_east[...] = acc[:, 12:15, 12:16, :]
    for copy in copies:
        copy.wait()


def inner_rows(off_one, off_two, grow_two, shrink_two, *operands):
    states = [jax.ShapeDtypeStruct((9, 36, 4, C), F32)] * 2
    smem = pl.BlockSpec(memory_space=pltpu.SMEM)
    return pl.pallas_call(
        inner_kernel,
        out_shape=states
        + results([(9, 9, 16, C), (9, 3, 4, C), (9, 3, 4, C), (9, 9, 16, 384)])
        + results([(640, 384), (C, 1152)], BF16),
        in_specs=[smem, smem] + [HBM] * 2 + vmem(11),
        out_specs=[HBM] * 2 + vmem(6),
        scratch_shapes=[
            pltpu.VMEM((9, 15, 16, C), F32),
            pltpu.VMEM((2, 3, 36, 4, C), F32),
            pltpu.VMEM((384, 384), F32),
            pltpu.VMEM((C, 384), F32),
            pltpu.VMEM((640, 384), BF16),
            pltpu.SemaphoreType.DMA((8,)),
        ],
        name="inner_rows",
        compiler_params=params(16),
    )(off_one, off_two, *far_off(grow_two, shrink_two), *operands)


def all_columns_kernel(
    from_top, from_bottom, acc_mid, checks_q, checks_g, g2m, s2, fresh, edge_m, edge_h, edge_g, acc
):
    acc[...] = acc_mid[...]
    for q in range(4):
        sub = slice(4 * q, 4 * q + 4)
        cols = slice(3 + 9 * q, 12 + 9 * q)
        acc[0:3, :, sub, :] = acc[0:3, :, sub, :] + from_top[:, cols]
        acc[6:9, :, sub, :] = acc[6:9, :, sub, :] + from_bottom[:, cols]
    for edge, whole in ((edge_m, acc), (edge_h, checks_q), (edge_g, checks_g)):
        edge[:, :, 0:4, :] = whole[:, 0:3, 0:4, :]
        edge[:, :, 4:8, :] = whole[:, 6:9, 12:16, :]
    groups = (slice(0, 5), slice(5, 9))
    news = together(
        *(
            update(checks_q[r].reshape(-1, C), checks_g[r].reshape(-1, 384), acc[r].reshape(-1, C), g2m, s2)
            for r in groups
        )
    )
    for rows, new in zip(groups, news):
        to_sites(fresh.at[rows], new.reshape(-1, 9, 16, C))


def all_columns(*operands):
    return pl.pallas_call(
        all_columns_kernel,
        out_shape=results([(9, 36, 4, C), (9, 3, 8, C), (9, 3, 8, C), (9, 3, 8, 384)]),
        in_specs=vmem(7),
        out_specs=vmem(4),
        scratch_shapes=[pltpu.VMEM((9, 9, 16, C), F32)],
        name="all_columns",
        compiler_params=params(14),
    )(*operands)


def edge_columns_kernel(far, near, states, edge_m, edge_h, edge_g, g2m, s2, out, message, fresh, sems):
    copies = [pltpu.make_async_copy(states.at[:, pl.ds(3, 30)], out.at[:, pl.ds(3, 30)], sems.at[2])]
    copies[0].start()
    message[...] = edge_m[...]
    odd = is_odd("gy") == 1
    message[:, :, 0:4, :] = message[:, :, 0:4, :] + jnp.where(odd, near[...], far[...])
    message[:, :, 4:8, :] = message[:, :, 4:8, :] + jnp.where(odd, far[...], near[...])
    (new,) = together(
        update(edge_h[...].reshape(216, C), edge_g[...].reshape(216, 384), message[...].reshape(216, C), g2m, s2)
    )
    new = new.reshape(9, 3, 8, C)
    for n, at in enumerate((0, 33)):
        fresh[n] = new[:, :, 4 * n : 4 * n + 4, :]
        copies.append(pltpu.make_async_copy(fresh.at[n], out.at[:, pl.ds(at, 3)], sems.at[n]))
        copies[-1].start()
    for copy in copies:
        copy.wait()


def edge_columns(*operands):
    return pl.pallas_call(
        edge_columns_kernel,
        out_shape=jax.ShapeDtypeStruct((9, 36, 4, C), F32),
        in_specs=vmem(8),
        out_specs=HBM,
        scratch_shapes=[
            pltpu.VMEM((9, 3, 8, C), F32), pltpu.VMEM((2, 9, 3, 4, C), F32), pltpu.SemaphoreType.DMA((3,)),
        ],
        name="edge_columns",
        compiler_params=params(8),
    )(*operands)


def trade(near, far, axis):
    count = lax.axis_size(axis)
    beyond = [(i, (i + (1 if i % 2 else -1)) % count) for i in range(count)]
    got = lax.ppermute(far, axis, beyond)
    return lax.ppermute(near, axis, [(i, i ^ 1) for i in range(count)]), got


def body(
    check_state, syndrome, left_state, right_state, offsets_one, offsets_two, syndrome_gain,
    mix_one, grow_one, shrink_one, mix_two, grow_two, shrink_two,
):
    site = lambda x: jnp.transpose(x, (1, 2, 0, 3))
    back = lambda x: jnp.transpose(x, (2, 0, 1, 3))
    check, bits, gain = site(check_state), jnp.transpose(syndrome, (1, 0, 2)), syndrome_gain.reshape(1, C)
    far, near, first, last = make_edges(check, bits, gain)
    near, far = trade(near, far, "gx")
    middle, m1, g1m, s1, m2, left_q, right_q, checks_q, left_g, right_g, pairs, acc = prework(
        check, bits, gain, site(left_state), site(right_state),
        mix_one, grow_one, jnp.swapaxes(shrink_one, 1, 2), mix_two, first, last,
    )
    near, far, middle = lax.optimization_barrier((near, far, middle))
    far, near, top, bottom = make_columns(near, far, first, middle, last)
    near, far = trade(near, far, "gy")
    steps = (offsets_one.T, offsets_two.T)
    shared = (left_q, right_q, left_g, right_g, m1, g1m, s1, m2)
    pairs, acc, *core = core_columns(*steps, pairs, acc, first, middle, last, top, bottom, *shared)
    pairs, acc, far, near, states = outer_rows(*steps, pairs, acc, far, near, *core, *shared)
    near, far = trade(near, far, "gx")
    left_out, right_out, acc_mid, acc_west, acc_east, checks_g, g2m, s2 = inner_rows(
        *steps, grow_two, shrink_two.T, pairs, acc, states, *shared
    )
    near, far, acc_mid = lax.optimization_barrier((near, far, acc_mid))
    far, near, from_top, from_bottom = make_sums(near, far, acc_west, acc_east)
    near, far = trade(near, far, "gy")
    states, edge_m, edge_h, edge_g = all_columns(from_top, from_bottom, acc_mid, checks_q, checks_g, g2m, s2)
    check_out = edge_columns(far, near, states, edge_m, edge_h, edge_g, g2m, s2)
    return back(left_out), back(right_out), back(check_out)


def solution(mesh):
    site = P(None, "gx", "gy", None)
    in_specs = (site, P(None, "gx", "gy"), site, site) + (P(),) * 9
    return jax.shard_map(body, mesh=mesh, in_specs=in_specs, out_specs=(site,) * 3, check_vma=False)
```

```python
import jax
import jax.numpy as jnp
from jax import lax
from jax.experimental import pallas as pl
from jax.experimental.pallas import tpu as pltpu
from jax.sharding import PartitionSpec as P

SPAN = 3
C = 192
F32 = jnp.float32
BF16 = jnp.bfloat16


def split(x):
    hi = x.astype(BF16)
    lo = (x - hi.astype(F32)).astype(BF16)
    return hi, lo


def packed(x):
    first, rest = x[:, :128], x[:, 128:]
    hi, lo = split(first)
    twice = jnp.concatenate([rest, rest], axis=1)
    rest_hi = twice.astype(BF16).astype(F32)
    lane = lax.broadcasted_iota(jnp.int32, twice.shape, 1)
    both = jnp.where(lane < 64, rest_hi, twice - rest_hi).astype(BF16)
    return [hi, both, lo]


def dot(a, b):
    return lax.dot_general(a, b, (((1,), (0,)), ((), ())), preferred_element_type=F32)


def dot_t(a, b):
    return lax.dot_general(a, b, (((1,), (1,)), ((), ())), preferred_element_type=F32)


def silu(v):
    return 0.5 * v * (1.0 + jnp.tanh(0.5 * v))


def vmem(count):
    return [pl.BlockSpec(memory_space=pltpu.VMEM)] * count


def params(mib):
    return pltpu.CompilerParams(vmem_limit_bytes=mib * 1024 * 1024)


HBM = pl.BlockSpec(memory_space=pltpu.HBM)


def far_off(*arrays):
    return [pltpu.with_memory_space_constraint(x, pltpu.HBM) for x in arrays]


def results(shapes, kind=F32):
    return [jax.ShapeDtypeStruct(shape, kind) for shape in shapes]


def fetch(pairs, sems):
    copies = [pltpu.make_async_copy(src, dst, sems.at[i]) for i, (src, dst) in enumerate(pairs)]
    for copy in copies:
        copy.start()
    return copies


def pair_rows(out, weights):
    hi, lo = split(weights)
    n = weights.shape[1]
    out[0:192, :n] = hi
    out[192:256, :n] = hi[128:192]
    out[256:384, :n] = hi[0:128]
    return lo


def low_rows(out, lo):
    n = lo.shape[1]
    out[0:192, :n] = lo
    out[192:256, :n] = jnp.zeros((64, n), BF16)


def picker():
    column = lax.broadcasted_iota(jnp.int32, (36, 8, 36), 0)
    lane = lax.broadcasted_iota(jnp.int32, (36, 8, 36), 2)
    return (column == lane).astype(F32)


def gains_row(syndrome, gain, pick):
    bits = (2 * syndrome - 1).astype(F32)
    bits = jnp.concatenate([bits, bits], axis=0)
    sign = jnp.sum(pick * bits[None], axis=-1, keepdims=True)[:, 0:4, :]
    return sign * gain


def is_odd(axis="gx"):
    return lax.rem(lax.axis_index(axis), 2)


def dense(value):
    half = value.shape[1] // 2
    rest = jnp.concatenate([value[:, :half, :, 128:], value[:, half:, :, 128:]], axis=-1)
    return jnp.concatenate([value[:, :, :, :128], rest], axis=1)


def undense(out, ref):
    columns = out.shape[1]
    half = columns // 2
    out[:, :, :, :128] = ref[:, :columns]
    out[:, :half, :, 128:] = ref[:, columns:, :, :64]
    out[:, half:, :, 128:] = ref[:, columns:, :, 64:]


def edges_kernel(check, syndrome, gain, far, near, first, last, rows, bits, gains, sems):
    copies = fetch(
        [(syndrome, bits), (gain, gains)] + [(check.at[pl.ds(r, 3)], rows.at[pl.ds(r, 3)]) for r in (0, 6)], sems
    )
    pick = picker()
    copies[0].wait()
    copies[1].wait()
    for r in range(3):
        first[r] = gains_row(bits[r], gains[...], pick)
        last[r] = gains_row(bits[6 + r], gains[...], pick)
    copies[2].wait()
    first[...] = first[...] + rows[0:3]
    copies[3].wait()
    last[...] = last[...] + rows[6:9]
    odd = is_odd() == 1
    low, high = dense(first[...]), dense(last[...])
    near[...] = jnp.where(odd, low, high)
    far[...] = jnp.where(odd, high, low)


def make_edges(check, syndrome, gain):
    return pl.pallas_call(
        edges_kernel,
        out_shape=results([(3, 54, 4, 128)] * 2 + [(3, 36, 4, C)] * 2),
        in_specs=[HBM] * 3,
        out_specs=vmem(4),
        scratch_shapes=[
            pltpu.VMEM((9, 36, 4, C), F32), pltpu.VMEM((9, 4, 36), jnp.int32), pltpu.VMEM((1, C), F32),
            pltpu.SemaphoreType.DMA((4,)),
        ],
        name="edges",
        compiler_params=params(8),
    )(*far_off(check, syndrome, gain))


def grow(src, out_h, out_m):
    for at, out in ((0, out_h), (192, out_m)):
        low_rows(out.at[384:640], pair_rows(out.at[0:384], src[at : at + 192, :]))


def shrink(src, out):
    hi, lo = split(src[...])
    out[:, 0:384] = hi
    out[:, 384:768] = hi
    out[:, 768:1152] = lo


def prework_kernel(
    check, syndrome, gain, left, right, mix_one, grow_one, shrink_one, mix_two, first, last,
    middle, m1, g1m, s1, m2, left_q, right_q, checks_q, left_g, right_g, pairs, acc,
    g1h, rows, bits, gains, lefts, rights, mix_1, grow_1, shrink_1, mix_2, sems,
):
    copies = fetch(
        [
            (left, lefts), (grow_one, grow_1), (right, rights), (mix_one, mix_1), (mix_two, mix_2),
            (shrink_one, shrink_1), (syndrome, bits), (gain, gains), (check.at[3:6], rows),
        ],
        sems,
    )

    def mixes(b):
        for k in range(3):
            low = pair_rows(m1.at[b, 384 * k : 384 * k + 384], mix_1[3 * b + k])
            low_rows(m1.at[b, 1152 + 256 * k : 1408 + 256 * k], low)
            out = m2.at[b, :, 256 * k : 256 * k + 256]
            low_rows(out.at[384:640], pair_rows(out.at[0:384], mix_2[3 * b + k]))

    def half(b, ref, quart, out):
        copies[2 * b].wait()
        for q in range(4):
            quart[:, :, 4 * q : 4 * q + 4, :] = ref[:, 9 * q : 9 * q + 9]
        if b == 0:
            copies[1].wait()
        grow(grow_1.at[b], g1h.at[b], g1m.at[b])
        tiles = packed(quart[...].reshape(1296, C))
        yield
        out[...] = dot(jnp.concatenate(tiles + tiles[:2], axis=1), g1h[b]).reshape(9, 9, 16, 384)
        if b == 0:
            for copy in copies[3:6]:
                copy.wait()
        mixes(b)
        shrink(shrink_1.at[b], s1.at[b])
        yield

    def checks():
        yield
        for copy in copies[6:]:
            copy.wait()
        pick = picker()
        for r in range(3):
            middle[r] = rows[r] + gains_row(bits[3 + r], gains[...], pick)
        for r, ref in enumerate((first, middle, last)):
            for q in range(4):
                checks_q[3 * r : 3 * r + 3, :, 4 * q : 4 * q + 4, :] = ref[:, 9 * q : 9 * q + 9]
        tiles = packed(checks_q[...].reshape(1296, C))
        for t in range(3):
            pairs[3:12, 3:12, :, 128 * t : 128 * t + 128] = tiles[t].reshape(9, 9, 16, 128)
        acc[...] = jnp.zeros(acc.shape, F32)

    together(half(0, lefts, left_q, left_g), half(1, rights, right_q, right_g), checks())


def prework(*operands):
    weights = [(2, 1920, C), (2, 640, 384), (2, C, 1152), (2, 640, 768)]
    states = [(9, 9, 16, C)] * 3 + [(9, 9, 16, 384)] * 2
    scratch = [(3, 36, 4, C), (9, 4, 36), (1, C), (9, 36, 4, C), (9, 36, 4, C), (6, C, C), (2, 384, 384)]
    scratch += [(2, C, 384), (6, C, C)]
    return pl.pallas_call(
        prework_kernel,
        out_shape=results([(3, 36, 4, C)])
        + results(weights, BF16)
        + results(states)
        + results([(15, 15, 16, 384)], BF16)
        + results([(15, 15, 16, C)]),
        in_specs=[HBM] * 9 + vmem(2),
        out_specs=vmem(12),
        scratch_shapes=[pltpu.VMEM((2, 640, 384), BF16)]
        + [pltpu.VMEM(s, jnp.int32 if s == (9, 4, 36) else F32) for s in scratch]
        + [pltpu.SemaphoreType.DMA((9,))],
        name="prework",
        compiler_params=params(18),
    )(*far_off(*operands[:9]), *operands[9:])


def columns_kernel(near, far, first, middle, last, to_far, to_near, beyond, low, high):
    odd = is_odd()
    undense(beyond.at[1 - odd], near)
    undense(beyond.at[odd], far)
    top, bottom = beyond.at[0], beyond.at[1]
    for r, ref in enumerate((top, first, middle, last, bottom)):
        low[3 * r : 3 * r + 3] = ref[:, 0:3]
        high[3 * r : 3 * r + 3] = ref[:, 33:36]
    odd = is_odd("gy") == 1
    to_far[...] = jnp.where(odd, high[...], low[...])
    to_near[...] = jnp.where(odd, low[...], high[...])


def make_columns(*operands):
    return pl.pallas_call(
        columns_kernel,
        out_shape=results([(15, 3, 4, C)] * 2 + [(2, 3, 36, 4, C)]),
        in_specs=vmem(5),
        out_specs=vmem(3),
        scratch_shapes=[pltpu.VMEM((15, 3, 4, C), F32)] * 2,
        name="columns",
        compiler_params=params(6),
    )(*operands)


def sums_kernel(near, far, acc_west, acc_east, to_far, to_near, beyond, low, high):
    odd = is_odd()
    undense(beyond.at[1 - odd], near)
    undense(beyond.at[odd], far)
    top, bottom = beyond.at[0], beyond.at[1]
    for ref, acc, cols in ((low, acc_west, slice(0, 3)), (high, acc_east, slice(39, 42))):
        ref[0:3] = acc[0:3] + top[:, cols]
        ref[3:6] = acc[3:6]
        ref[6:9] = acc[6:9] + bottom[:, cols]
    odd = is_odd("gy") == 1
    to_far[...] = jnp.where(odd, high[...], low[...])
    to_near[...] = jnp.where(odd, low[...], high[...])


def make_sums(*operands):
    return pl.pallas_call(
        sums_kernel,
        out_shape=results([(9, 3, 4, C)] * 2 + [(2, 3, 42, 4, C)]),
        in_specs=vmem(4),
        out_specs=vmem(3),
        scratch_shapes=[pltpu.VMEM((9, 3, 4, C), F32)] * 2,
        name="sums",
        compiler_params=params(6),
    )(*operands)


def update(h, half, m, grow, shrink):
    mean = jnp.sum(h * h + m * m, axis=-1, keepdims=True) * (1.0 / 384.0)
    mp = packed(m)
    yield
    grown = dot(jnp.concatenate(mp + mp[:2], axis=1), grow[...])
    yield
    hi, lo = split(silu((grown + half) * lax.rsqrt(mean + 1e-05)))
    yield
    yield h + dot_t(jnp.concatenate([hi, lo, hi], axis=1), shrink[...])


def together(*steps):
    last = [None] * len(steps)
    live = list(range(len(steps)))
    while live:
        for i in list(live):
            try:
                last[i] = next(steps[i])
            except StopIteration:
                live.remove(i)
    return last


def block_step(b, pieces, off_one, off_two, pairs, margin, state, half, m1, g1m, s1, m2, acc, base):
    sizes = [48 * wide for _, _, wide in pieces]

    def windows(ref, down=0, across=0):
        parts = [
            ref[pl.ds(row + down, 3), pl.ds(col + across, wide)].reshape(48 * wide, ref.shape[-1])
            for row, col, wide in pieces
        ]
        return jnp.concatenate(parts, axis=0)

    slabs = [
        windows(pairs, SPAN + off_one[0, 3 * b + k], margin + off_one[1, 3 * b + k]) for k in range(3)
    ]
    m = dot(jnp.concatenate(slabs + [s[:, :256] for s in slabs], axis=1), m1[b])
    yield
    for new in update(windows(state), windows(half), m, g1m.at[b], s1.at[b]):
        yield
    tiles = packed(new)
    yield
    parts = dot(jnp.concatenate(tiles + tiles[:2], axis=1), m2[b])
    yield
    for k in range(3):
        down, across = off_two[0, 3 * b + k], off_two[1, 3 * b + k]
        at = 0
        for size, (row, col, wide) in zip(sizes, pieces):
            where = (pl.ds(base + row - down, 3), pl.ds(SPAN + col - across, wide))
            acc[where] = acc[where] + parts[at : at + size, 256 * k : 256 * k + 192].reshape(3, wide, 16, C)
            at += size
    at, news = 0, []
    for size, (row, col, wide) in zip(sizes, pieces):
        news.append(new[at : at + size].reshape(3, wide, 16, C))
        at += size
    yield news


def layer_one_steps(pieces, off_one, off_two, pairs, margin, states, halves, m1, g1m, s1, m2, acc, base):
    return together(
        *(
            block_step(b, pieces, off_one, off_two, pairs, margin, states[b], halves[b], m1, g1m, s1, m2, acc, base)
            for b in range(2)
        )
    )


def to_sites(out, value, col=0):
    for q in range(4):
        out[:, 9 * q + col : 9 * q + col + value.shape[1]] = value[:, :, 4 * q : 4 * q + 4, :]


def fold(acc, rows):
    for q in range(3):
        low, high = slice(4 * q, 4 * q + 4), slice(4 * q + 4, 4 * q + 8)
        acc[rows, 3:6, high, :] = acc[rows, 3:6, high, :] + acc[rows, 12:15, low, :]
        acc[rows, 9:12, low, :] = acc[rows, 9:12, low, :] + acc[rows, 0:3, high, :]


def core_kernel(
    off_one, off_two, pairs_in, acc_in, first, middle, last, beyond, left_q, right_q, left_g, right_g,
    m1, g1m, s1, m2,
    pairs, acc, west_q, east_q, left_core, right_core,
    field,
):
    top, bottom = beyond.at[0], beyond.at[1]
    for at, ref in ((0, top), (12, bottom)):
        for q in range(4):
            field[:, :, 4 * q : 4 * q + 4, :] = ref[:, 9 * q : 9 * q + 9]
        tiles = packed(field[...].reshape(432, C))
        for t in range(3):
            pairs[at : at + 3, 3:12, :, 128 * t : 128 * t + 128] = tiles[t].reshape(3, 9, 16, 128)
    for r, ref in enumerate((top, first, middle, last, bottom)):
        for q in range(3):
            east_q[3 * r : 3 * r + 3, :, 4 * q : 4 * q + 4, :] = ref[:, 9 * q + 9 : 9 * q + 12]
            west_q[3 * r : 3 * r + 3, :, 4 * q + 4 : 4 * q + 8, :] = ref[:, 9 * q + 6 : 9 * q + 9]
    news = layer_one_steps(
        [(0, 3, 3), (6, 3, 3)], off_one, off_two, pairs, SPAN, (left_q, right_q), (left_g, right_g), m1, g1m, s1, m2,
        acc, SPAN,
    )
    for ref, (low, high) in zip((left_core, right_core), news):
        ref[0:3] = low
        ref[3:6] = high


IN_PLACE = [(15, 15, 16, 384), (15, 15, 16, C)]


def core_columns(off_one, off_two, *operands):
    smem = pl.BlockSpec(memory_space=pltpu.SMEM)
    shapes = [(15, 3, 16, C), (15, 3, 16, C), (6, 3, 16, C), (6, 3, 16, C)]
    return pl.pallas_call(
        core_kernel,
        out_shape=results(IN_PLACE[:1], BF16) + results(IN_PLACE[1:] + shapes),
        in_specs=[smem, smem] + vmem(14),
        out_specs=vmem(6),
        scratch_shapes=[pltpu.VMEM((3, 9, 16, C), F32)],
        input_output_aliases={2: 0, 3: 1},
        name="core_columns",
        compiler_params=params(12),
    )(off_one, off_two, *operands)


def outer_kernel(
    off_one, off_two, pairs_in, acc_in, far_in, near_in, west_q, east_q, left_core, right_core,
    left_q, right_q, left_g, right_g, m1, g1m, s1, m2,
    pairs, acc, far, near, fresh,
    side, whole,
):
    odd = is_odd("gy") == 1
    west = jnp.where(odd, near_in[...], far_in[...])
    east = jnp.where(odd, far_in[...], near_in[...])
    for at, known, new, sub in ((0, west_q, west, 0), (12, east_q, east, 12)):
        side[...] = known[...]
        side[:, :, sub : sub + 4, :] = new
        tiles = packed(side[...].reshape(720, C))
        for t in range(3):
            pairs[:, at : at + 3, :, 128 * t : 128 * t + 128] = tiles[t].reshape(15, 3, 16, 128)
    pieces = [(0, 0, 3), (0, 6, 3), (6, 0, 3), (6, 6, 3)]
    news = layer_one_steps(
        pieces, off_one, off_two, pairs, SPAN, (left_q, right_q), (left_g, right_g), m1, g1m, s1, m2, acc, SPAN
    )
    for b, (new, core) in enumerate(zip(news, (left_core, right_core))):
        to_sites(fresh.at[b], core[...], 3)
        for (row, col, _), value in zip(pieces, new):
            to_sites(fresh.at[b, row // 2 : row // 2 + 3], value, col)
    for n, at in enumerate((0, 12)):
        rows = slice(at, at + 3)
        fold(acc, rows)
        whole[n, :, 0:3] = acc[rows, 0:3, 0:4, :]
        to_sites(whole.at[n, :, 3:39], acc[rows, 3:12])
        whole[n, :, 39:42] = acc[rows, 12:15, 12:16, :]
    odd = is_odd()
    near[...] = dense(whole[1 - odd])
    far[...] = dense(whole[odd])


def outer_rows(off_one, off_two, *operands):
    smem = pl.BlockSpec(memory_space=pltpu.SMEM)
    shapes = [(3, 63, 4, 128), (3, 63, 4, 128), (2, 6, 36, 4, C)]
    return pl.pallas_call(
        outer_kernel,
        out_shape=results(IN_PLACE[:1], BF16) + results(IN_PLACE[1:] + shapes),
        in_specs=[smem, smem] + vmem(16),
        out_specs=vmem(5),
        scratch_shapes=[pltpu.VMEM((15, 3, 16, C), F32), pltpu.VMEM((2, 3, 42, 4, C), F32)],
        input_output_aliases={2: 0, 3: 1},
        name="outer_rows",
        compiler_params=params(14),
    )(off_one, off_two, *operands)


def inner_kernel(
    off_one, off_two, grow_two, shrink_two, pairs, acc_in, outer_states,
    left_q, right_q, left_g, right_g, m1, g1m, s1, m2,
    left_out, right_out, acc_mid, acc_west, acc_east, checks_g, g2m, s2,
    acc, fresh, grow_2, shrink_2, g2h, sems,
):
    loads = fetch([(grow_two, grow_2), (shrink_two, shrink_2)], sems)
    copies = [
        pltpu.make_async_copy(outer_states.at[b, pl.ds(at // 2, 3)], out.at[pl.ds(at, 3)], sems.at[2 + 3 * b + n])
        for b, out in enumerate((left_out, right_out))
        for n, at in enumerate((0, 6))
    ]
    for copy in copies:
        copy.start()
    acc[...] = acc_in[3:12]
    news = layer_one_steps(
        [(3, 0, 9)], off_one, off_two, pairs, SPAN, (left_q, right_q), (left_g, right_g), m1, g1m, s1, m2, acc, 0
    )
    for b, ((new,), out) in enumerate(zip(news, (left_out, right_out))):
        to_sites(fresh.at[b], new)
        copies.append(pltpu.make_async_copy(fresh.at[b], out.at[pl.ds(3, 3)], sems.at[4 + 3 * b]))
        copies[-1].start()
    for copy in loads:
        copy.wait()
    grow(grow_2, g2h, g2m)
    shrink(shrink_2, s2)
    tiles = pairs[3:12, 3:12].reshape(1296, 384)
    checks_g[...] = dot(jnp.concatenate([tiles, tiles[:, :256]], axis=1), g2h[...]).reshape(9, 9, 16, 384)
    fold(acc, slice(0, 9))
    acc_mid[...] = acc[:, 3:12]
    acc_west[...] = acc[:, 0:3, 0:4, :]
    acc_east[...] = acc[:, 12:15, 12:16, :]
    for copy in copies:
        copy.wait()


def inner_rows(off_one, off_two, grow_two, shrink_two, *operands):
    states = [jax.ShapeDtypeStruct((9, 36, 4, C), F32)] * 2
    smem = pl.BlockSpec(memory_space=pltpu.SMEM)
    return pl.pallas_call(
        inner_kernel,
        out_shape=states
        + results([(9, 9, 16, C), (9, 3, 4, C), (9, 3, 4, C), (9, 9, 16, 384)])
        + results([(640, 384), (C, 1152)], BF16),
        in_specs=[smem, smem] + [HBM] * 2 + vmem(11),
        out_specs=[HBM] * 2 + vmem(6),
        scratch_shapes=[
            pltpu.VMEM((9, 15, 16, C), F32),
            pltpu.VMEM((2, 3, 36, 4, C), F32),
            pltpu.VMEM((384, 384), F32),
            pltpu.VMEM((C, 384), F32),
            pltpu.VMEM((640, 384), BF16),
            pltpu.SemaphoreType.DMA((8,)),
        ],
        name="inner_rows",
        compiler_params=params(16),
    )(off_one, off_two, *far_off(grow_two, shrink_two), *operands)


def all_columns_kernel(
    beyond, acc_mid, checks_q, checks_g, g2m, s2, fresh, edge_m, edge_h, edge_g, acc
):
    from_top, from_bottom = beyond.at[0], beyond.at[1]
    acc[...] = acc_mid[...]
    for q in range(4):
        sub = slice(4 * q, 4 * q + 4)
        cols = slice(3 + 9 * q, 12 + 9 * q)
        acc[0:3, :, sub, :] = acc[0:3, :, sub, :] + from_top[:, cols]
        acc[6:9, :, sub, :] = acc[6:9, :, sub, :] + from_bottom[:, cols]
    for edge, whole in ((edge_m, acc), (edge_h, checks_q), (edge_g, checks_g)):
        edge[:, :, 0:4, :] = whole[:, 0:3, 0:4, :]
        edge[:, :, 4:8, :] = whole[:, 6:9, 12:16, :]
    groups = (slice(0, 5), slice(5, 9))
    news = together(
        *(
            update(checks_q[r].reshape(-1, C), checks_g[r].reshape(-1, 384), acc[r].reshape(-1, C), g2m, s2)
            for r in groups
        )
    )
    for rows, new in zip(groups, news):
        to_sites(fresh.at[rows], new.reshape(-1, 9, 16, C))


def all_columns(*operands):
    return pl.pallas_call(
        all_columns_kernel,
        out_shape=results([(9, 36, 4, C), (9, 3, 8, C), (9, 3, 8, C), (9, 3, 8, 384)]),
        in_specs=vmem(6),
        out_specs=vmem(4),
        scratch_shapes=[pltpu.VMEM((9, 9, 16, C), F32)],
        name="all_columns",
        compiler_params=params(14),
    )(*operands)


def edge_columns_kernel(far, near, states, edge_m, edge_h, edge_g, g2m, s2, out, message, fresh, sems):
    copies = [pltpu.make_async_copy(states.at[:, pl.ds(3, 30)], out.at[:, pl.ds(3, 30)], sems.at[2])]
    copies[0].start()
    message[...] = edge_m[...]
    odd = is_odd("gy") == 1
    message[:, :, 0:4, :] = message[:, :, 0:4, :] + jnp.where(odd, near[...], far[...])
    message[:, :, 4:8, :] = message[:, :, 4:8, :] + jnp.where(odd, far[...], near[...])
    (new,) = together(
        update(edge_h[...].reshape(216, C), edge_g[...].reshape(216, 384), message[...].reshape(216, C), g2m, s2)
    )
    new = new.reshape(9, 3, 8, C)
    for n, at in enumerate((0, 33)):
        fresh[n] = new[:, :, 4 * n : 4 * n + 4, :]
        copies.append(pltpu.make_async_copy(fresh.at[n], out.at[:, pl.ds(at, 3)], sems.at[n]))
        copies[-1].start()
    for copy in copies:
        copy.wait()


def edge_columns(*operands):
    return pl.pallas_call(
        edge_columns_kernel,
        out_shape=jax.ShapeDtypeStruct((9, 36, 4, C), F32),
        in_specs=vmem(8),
        out_specs=HBM,
        scratch_shapes=[
            pltpu.VMEM((9, 3, 8, C), F32), pltpu.VMEM((2, 9, 3, 4, C), F32), pltpu.SemaphoreType.DMA((3,)),
        ],
        name="edge_columns",
        compiler_params=params(8),
    )(*operands)


def trade(near, far, axis):
    count = lax.axis_size(axis)
    beyond = [(i, (i + (1 if i % 2 else -1)) % count) for i in range(count)]
    got = lax.ppermute(far, axis, beyond)
    return lax.ppermute(near, axis, [(i, i ^ 1) for i in range(count)]), got


def body(
    check_state, syndrome, left_state, right_state, offsets_one, offsets_two, syndrome_gain,
    mix_one, grow_one, shrink_one, mix_two, grow_two, shrink_two,
):
    site = lambda x: jnp.transpose(x, (1, 2, 0, 3))
    back = lambda x: jnp.transpose(x, (2, 0, 1, 3))
    check, bits, gain = site(check_state), jnp.transpose(syndrome, (1, 0, 2)), syndrome_gain.reshape(1, C)
    far, near, first, last = make_edges(check, bits, gain)
    near, far = trade(near, far, "gx")
    middle, m1, g1m, s1, m2, left_q, right_q, checks_q, left_g, right_g, pairs, acc = prework(
        check, bits, gain, site(left_state), site(right_state),
        mix_one, grow_one, jnp.swapaxes(shrink_one, 1, 2), mix_two, first, last,
    )
    near, far, middle = lax.optimization_barrier((near, far, middle))
    far, near, rows = make_columns(near, far, first, middle, last)
    near, far = trade(near, far, "gy")
    steps = (offsets_one.T, offsets_two.T)
    shared = (left_q, right_q, left_g, right_g, m1, g1m, s1, m2)
    pairs, acc, *core = core_columns(*steps, pairs, acc, first, middle, last, rows, *shared)
    pairs, acc, far, near, states = outer_rows(*steps, pairs, acc, far, near, *core, *shared)
    near, far = trade(near, far, "gx")
    left_out, right_out, acc_mid, acc_west, acc_east, checks_g, g2m, s2 = inner_rows(
        *steps, grow_two, shrink_two.T, pairs, acc, states, *shared
    )
    near, far, acc_mid = lax.optimization_barrier((near, far, acc_mid))
    far, near, rows = make_sums(near, far, acc_west, acc_east)
    near, far = trade(near, far, "gy")
    states, edge_m, edge_h, edge_g = all_columns(rows, acc_mid, checks_q, checks_g, g2m, s2)
    check_out = edge_columns(far, near, states, edge_m, edge_h, edge_g, g2m, s2)
    return back(left_out), back(right_out), back(check_out)


def solution(mesh):
    site = P(None, "gx", "gy", None)
    in_specs = (site, P(None, "gx", "gy"), site, site) + (P(),) * 9
    return jax.shard_map(body, mesh=mesh, in_specs=in_specs, out_specs=(site,) * 3, check_vma=False)
```
